256 devices in a mesh: dp: 8 (over y, core), queue: 32 (over z, x).
Axes of the slice: x: 4, y: 4, z: 8, core: 2. Of those that a mesh axis runs over, the one named last changes fastest.
Arguments:
- features: bfloat16 [131072, 1024], P(('dp', 'queue')), may hold values from -1 to 1
- weight: bfloat16 [1024, 256], replicated, may hold values from -2 to 2
- support_queue: bfloat16 [262144, 256], P('queue'), may hold values from -100 to 100
- owner_shard: int32 [131072, 1], P(('dp', 'queue')), may hold values from 0 to 31; in each aligned block of 512 rows (0 to 511, 512 to 1023, ...) at most 64 rows name the same one
- slot_row: int32 [131072], P(('dp', 'queue')), may hold values from 0 to 8191
- loss_weight: bfloat16 [131072], P(('dp', 'queue')), may hold values from 0.5 to 2
Outputs:
- grad_feats: bfloat16 [131072, 1024], P(('dp', 'queue'))
- grad_weight: float32 [1024, 256], replicated
The draws below stay inside these ranges and needn't reach their ends.
Inputs may be any that keep to these rules, and one draw needn't show every extreme that they name: `owner_shard`: among the rows of one device no shard is named by more than 64 rows, a bound that some block reaches.
All inputs are finite; a program needn't handle non-finite values.
Results may differ from the reference program's by a relative error of at most 0.0035.
Values may be sent and summed in bfloat16 or wider, within the bound.
No kernel may reach another device: no remote copies, remote signals or barrier semaphores. Data moves between devices by JAX's collectives and lax.ppermute only.
A program may use at most 128 MiB of HBM per device.

```python
import math
import jax
import jax.numpy as jnp
import numpy as np
from jax import lax

D = 1024
E = 256
V_DEV = 512
QROWS_DEV = 8192
CAP = 64
GROUP = 16384
VIEWS = 131072
QROWS = 262144
N_DP = 8
N_QUEUE = 32


def shared_centres(key):
    return jnp.clip(jax.random.normal(key, (16, E), jnp.float32), -4.0, 4.0)


def draw_support_queue(key, part):
    centres = shared_centres(key)
    key = jax.random.fold_in(key, 5)
    member = jax.random.randint(jax.random.fold_in(key, 1), (QROWS,), 0, 16)
    located = 2.0 * centres[member]
    noise = jnp.clip(jax.random.normal(jax.random.fold_in(key, 2), (QROWS, E), jnp.float32), -4.0, 4.0)
    return (noise + located).astype(jnp.bfloat16)


def draw_weight(key, part):
    centres = shared_centres(key)
    key = jax.random.fold_in(key, 7)
    noise = jnp.clip(jax.random.normal(jax.random.fold_in(key, 1), (D, E), jnp.float32), -4.0, 4.0)
    gains = jnp.clip(jax.random.normal(jax.random.fold_in(key, 2), (D, 1), jnp.float32), -2.0, 2.0)
    picked = centres[jnp.arange(D, dtype=jnp.int32) % 16]
    return ((noise + 2.0 * gains * picked) * (1.0 / math.sqrt(5.0 * D))).astype(jnp.bfloat16)


def with_ends(values, own_key, smallest, high):
    longest = values.shape.index(max(values.shape))
    spots = []
    for shift in (0, 1):
        where = [jax.random.randint(jax.random.fold_in(own_key, axis), (), 0, length) for axis, length in enumerate(values.shape)]
        where[longest] = (where[longest] + shift) % values.shape[longest]
        spots.append(tuple(where))
    return values.at[spots[0]].set(smallest).at[spots[1]].set(high)


def strengthened(entries, stream_key, source, target, parts, factor):
    def block_of(dim):
        return (jnp.arange(entries.shape[dim]) // (entries.shape[dim] // parts)).reshape((-1,) + (1,) * (entries.ndim - 1 - dim))

    first = jax.random.permutation(stream_key, parts)[block_of(target)]
    second = (block_of(target) + parts // 2) % parts
    return jnp.where((block_of(source) == first) | (block_of(source) == second), factor * entries, entries)


def levels(stream_key, extent, shards, least, high):
    loudness = 1.0
    for dim, parts in shards:
        steps = jax.random.uniform(jax.random.fold_in(jax.random.fold_in(stream_key, 6), dim), (parts,), jnp.float32, least / len(shards), high / len(shards))
        loudness = loudness * jnp.repeat(jnp.exp(steps), extent[dim] // parts).reshape((-1,) + (1,) * (len(extent) - 1 - dim))
    return loudness


def deal_out(rng, own, number, rows, number_of, top, bound, lean):
    order = jax.random.permutation(rng, number_of)
    crowded, usual = shares(number_of, rows * top, bound, lean, True), shares(number_of, rows * top, bound, lean, False)
    places = jnp.arange(number_of)

    def named(tallies, offset_by):
        used = int((tallies > 0).sum())
        fixed = max(1, used // 4)
        shifted = fixed + (places - fixed + offset_by * (used - fixed)) % max(1, number_of - fixed)
        return jnp.zeros((number_of,), jnp.int32).at[order[jnp.where(places < fixed, places, shifted)]].set(jnp.asarray(tallies, jnp.int32))

    tallies = jnp.where(number % 4 == 0, named(crowded, number // 4), named(usual, number - number // 4 - 1))
    mixed = jax.random.permutation(jax.random.fold_in(own, 3), number_of)
    donor, sink = mixed[0:number_of // 2 * 2:2], mixed[1:number_of // 2 * 2:2]
    margin = jnp.minimum(tallies[donor] - 1, bound - tallies[sink]) // 2
    margin = jnp.where((donor == order[0]) | (sink == order[0]) | (tallies[sink] == 0), 0, jnp.maximum(margin, 0))
    shifted = jax.random.randint(jax.random.fold_in(own, 4), (number_of // 2,), 0, 1 << 20) % (margin + 1)
    tallies = tallies.at[donor].add(-shifted).at[sink].add(shifted)
    items = jnp.searchsorted(jnp.cumsum(tallies), jnp.arange(rows * top), side="right").astype(jnp.int32)
    grid = items.reshape(top, rows).T
    grid = grid[jax.random.permutation(jax.random.fold_in(own, 1), rows)]
    offset_by = jax.random.randint(jax.random.fold_in(own, 2), (rows, 1), 0, top)
    return jnp.take_along_axis(grid, (jnp.arange(top)[None, :] + offset_by) % top, axis=1)


def shares(count, total, reach, lean, full):
    portions = [(1 << 20) // math.isqrt(standing ** lean) + 1 for standing in range(1, count + 1)]
    largest = reach if full else min(reach, max(-(-total // count), total * portions[0] // sum(portions)))
    least = 1 if total - largest >= count - 1 else 0
    counts, rest = [largest] + [least] * (count - 1), total - largest - least * (count - 1)
    while rest > 0:
        movable = [i for i in range(1, count) if counts[i] < largest] or [i for i in range(1, count) if counts[i] < reach]
        mass, left = sum([portions[i] for i in movable]), rest
        for i in movable:
            extra = min(reach - counts[i], max(1, left * portions[i] // mass), rest)
            counts[i] = counts[i] + extra
            rest = rest - extra
    return np.array(counts)


def heavy_noise(own_key, shape, width, bound, cuts, heavy, kind=jnp.bfloat16):
    result = width * jax.random.normal(own_key, shape, jnp.float32)
    if cuts:
        result = result * levels(own_key, shape, cuts, -0.22, 0.18)
    return jnp.clip(strengthened(result, jax.random.fold_in(own_key, 3), *heavy), -bound, bound).astype(kind)


def setup_inputs(seed: int = 0) -> dict:
    streams_of = jax.random.split(jax.random.key(seed), 7)
    features = heavy_noise(streams_of[0], (VIEWS, D), 0.0625, 1.0, ((0, 256),), (0, 1, 256, 6.0))
    weight = draw_weight(jax.random.fold_in(streams_of[6], 71), 0)
    support_queue = draw_support_queue(jax.random.fold_in(streams_of[6], 71), 0)
    owner_shard_keys = jax.random.split(jax.random.fold_in(streams_of[3], 1), VIEWS // V_DEV)
    owner_shard_turns = jax.random.permutation(jax.random.fold_in(streams_of[3], 3), VIEWS // V_DEV)
    owner_shard = jax.vmap(lambda own, number: deal_out(jax.random.fold_in(streams_of[3], 2), own, number, V_DEV, N_QUEUE, 1, CAP, 2))(owner_shard_keys, owner_shard_turns).reshape((VIEWS, 1))
    slot_row = with_ends(jax.random.randint(streams_of[4], (VIEWS,), 0, QROWS_DEV), jax.random.fold_in(streams_of[4], 1), 0, QROWS_DEV - 1).astype(jnp.int32)
    loss_weight = jnp.clip(jnp.exp(math.log(2.0) - 1.3862944 * jax.random.uniform(streams_of[5], (VIEWS,), jnp.float32) ** levels(streams_of[5], (VIEWS,), ((0, 256),), -0.2, 0.2)), 0.5, 2.0).astype(jnp.bfloat16)
    return dict(features=features, weight=weight, support_queue=support_queue, owner_shard=owner_shard, slot_row=slot_row, loss_weight=loss_weight)


TEMPER = 0.1
EPSILON = 1e-06

def unit_rows(values):
    return values * lax.rsqrt(lax.optimization_barrier(jnp.sum(values * values, axis=-1, keepdims=True)) + EPSILON)

def group_grads(triple):
    anchors, embedded, weights = triple
    row_count = anchors.shape[0]
    logits = jnp.dot(anchors, embedded.T, preferred_element_type=jnp.float32) * (1.0 / TEMPER)
    exponent = jnp.exp(logits)
    totals = lax.optimization_barrier(jnp.sum(exponent, axis=1))
    chance = exponent / totals[:, None]
    weights = weights.astype(jnp.float32)
    weighted = weights[:, None] * chance
    places = jnp.arange(row_count)
    weighted = weighted.at[places, places].add(-weights)
    scaled = weighted.astype(jnp.bfloat16)
    return jnp.dot(scaled.T, anchors, preferred_element_type=jnp.float32) * (1.0 / TEMPER)

def reference(features, weight, support_queue, owner_shard, slot_row, loss_weight):
    projected = jnp.dot(features, weight, preferred_element_type=jnp.float32)
    inv_norm = lax.rsqrt(lax.optimization_barrier(jnp.sum(projected * projected, axis=1, keepdims=True)) + EPSILON)
    unit_view = projected * inv_norm
    view_bf = unit_view.astype(jnp.bfloat16)
    wanted = (owner_shard[:, 0] * QROWS_DEV + slot_row).astype(jnp.int32)
    anchors = unit_rows(support_queue[wanted].astype(jnp.float32)).astype(jnp.bfloat16)
    grads = lax.map(group_grads, (anchors.reshape(N_DP, GROUP, E), view_bf.reshape(N_DP, GROUP, E), loss_weight.reshape(N_DP, GROUP)))
    grad_unit = grads.reshape(VIEWS, E)
    grad_proj = (grad_unit - unit_view * lax.optimization_barrier(jnp.sum(unit_view * grad_unit, axis=1, keepdims=True))) * inv_norm
    grad_proj_bf = grad_proj.astype(jnp.bfloat16)
    grad_feats = jnp.dot(grad_proj_bf, weight.T, preferred_element_type=jnp.float32).astype(jnp.bfloat16)
    grad_weight = jnp.dot(features.T, grad_proj_bf, preferred_element_type=jnp.float32)
    return (grad_feats, grad_weight)
```

```python
import functools

import jax
import jax.numpy as jnp
from jax import lax
from jax.experimental import pallas as pl
from jax.experimental.pallas import tpu as pltpu
from jax.sharding import PartitionSpec as P

TEMPER = 0.1
EPSILON = 1e-06
NZ, NX, NY, NC = 8, 4, 4, 2
CAP = 64
BF = jnp.bfloat16
F32 = jnp.float32
VMEM_LIMIT = 48 * 1024 * 1024


def x_pairs(s):
    return [(z * NX + x, z * NX + (x + s) % NX) for z in range(NZ) for x in range(NX)]


def z_pairs(s):
    return [(z * NX + x, ((z + s) % NZ) * NX + x) for z in range(NZ) for x in range(NX)]


def z_flip(m):
    return [(z * NX + x, (z ^ m) * NX + x) for z in range(NZ) for x in range(NX)]


def y_pairs(s):
    return [(y * NC + c, ((y + s) % NY) * NC + c) for y in range(NY) for c in range(NC)]


CORE_PAIRS = [(d, d ^ 1) for d in range(NY * NC)]


def vmem_call(kernel, out_shape, name, limit=VMEM_LIMIT, **kw):
    return pl.pallas_call(
        kernel,
        out_shape=out_shape,
        compiler_params=pltpu.CompilerParams(vmem_limit_bytes=limit),
        name=name,
        **kw,
    )


def plan_kernel(owner_ref, slot_ref, wanted_ref, places_ref):
    n = owner_ref.shape[0]
    owner = owner_ref[...]
    slot = slot_ref[...]
    shard = lax.broadcasted_iota(jnp.int32, (n, 128), 1)
    onehot = (owner == shard).astype(F32)
    below = (
        lax.broadcasted_iota(jnp.int32, (n, n), 1) < lax.broadcasted_iota(jnp.int32, (n, n), 0)
    ).astype(F32).astype(BF)
    before = jnp.dot(below, onehot.astype(BF), preferred_element_type=F32)
    rank = jnp.sum(before * onehot, axis=1, keepdims=True).astype(jnp.int32)
    places_ref[...] = owner * CAP + rank
    chosen = rank == lax.broadcasted_iota(jnp.int32, (n, 128), 1)
    high = jnp.where(chosen, (slot >> 7).astype(F32), 0.0).astype(BF)
    low = jnp.where(chosen, (slot & 127).astype(F32), 0.0).astype(BF)
    across = (((0,), (0,)), ((), ()))
    hot = onehot.astype(BF)
    upper = lax.dot_general(hot, high, across, preferred_element_type=F32)
    lower = lax.dot_general(hot, low, across, preferred_element_type=F32)
    full = upper.astype(jnp.int32) * 128 + lower.astype(jnp.int32)
    wanted_ref[...] = full[: wanted_ref.shape[0], :CAP]


def plan(owner, slot):
    n = owner.shape[0]
    return vmem_call(
        plan_kernel,
        (
            jax.ShapeDtypeStruct((NZ * NX, CAP), jnp.int32),
            jax.ShapeDtypeStruct((n, 1), jnp.int32),
        ),
        "plan",
    )(owner, slot)


def unit_rows(values):
    return values * lax.rsqrt(jnp.sum(values * values, axis=-1, keepdims=True) + EPSILON)


def exps_kernel(blocks, *refs):
    anchors = refs[:blocks]
    views = refs[blocks : blocks + NZ]
    e_ref, t_ref = refs[blocks + NZ :]
    n = views[0].shape[0]
    for b in range(blocks):
        a = anchors[b][:n, :]
        total = jnp.zeros((1, n), F32)
        for k in range(NZ):
            dots = lax.dot_general(
                views[k][...], a, (((1,), (1,)), ((), ())), preferred_element_type=F32
            )
            e = jnp.exp(dots * (1.0 / TEMPER))
            total = total + jnp.sum(e, axis=0, keepdims=True)
            e_ref[k, :, b * n : (b + 1) * n] = e.astype(BF)
        t_ref[:, b * n : (b + 1) * n] = total


def exps(anchors, views):
    n = views[0].shape[0]
    blocks = len(anchors)
    return vmem_call(
        functools.partial(exps_kernel, blocks),
        (
            jax.ShapeDtypeStruct((NZ, n, blocks * n), BF),
            jax.ShapeDtypeStruct((1, blocks * n), F32),
        ),
        "exps",
    )(*anchors, *views)


def scale_kernel(*refs):
    anchors = refs[:NX]
    totals = refs[NX : 2 * NX]
    out_ref = refs[2 * NX]
    n = out_ref.shape[0] // NX
    width = out_ref.shape[1]
    for b in range(NX):
        t = None
        for k in range(NX):
            at = ((b - k) % NX) * n
            piece = totals[k][:, at : at + n]
            t = piece if t is None else t + piece
        w = anchors[b][n : n + 16, :].astype(F32)
        w = jnp.concatenate([w[k : k + 1, :] for k in range(n // width)], axis=1)
        c = (1.0 / TEMPER) * w / t
        column = jnp.broadcast_to(c, (8, n)).T[:, :1]
        out_ref[b * n : (b + 1) * n, :] = (anchors[b][:n, :].astype(F32) * column).astype(BF)


def scale(anchors, totals, n):
    return vmem_call(
        scale_kernel,
        jax.ShapeDtypeStruct((NX * n, anchors[0].shape[1]), BF),
        "scale",
    )(*anchors, *totals)


def mix_kernel(blocks, a_ref, *refs):
    parts, out_ref = refs[:blocks], refs[blocks]
    at = 0
    total = None
    for part in parts:
        size = part.shape[2]
        term = jnp.dot(part[0], a_ref[at : at + size, :], preferred_element_type=F32)
        total = term if total is None else total + term
        at += size
    out_ref[...] = total.astype(out_ref.dtype)


def mix(scaled, parts, k, dtype):
    n = parts[0].shape[1]
    width = scaled.shape[1]
    specs = [pl.BlockSpec((1, n, p.shape[2]), lambda i: (k, 0, 0)) for p in parts]
    return vmem_call(
        functools.partial(mix_kernel, len(parts)),
        jax.ShapeDtypeStruct((n, width), dtype),
        "mix",
        grid=(1,),
        in_specs=[pl.BlockSpec(scaled.shape, lambda i: (0, 0))] + specs,
        out_specs=pl.BlockSpec((n, width), lambda i: (0, 0)),
    )(scaled, *parts)


def block_of(v, index, rows):
    return lax.dynamic_slice(v, (index * rows, 0), (rows, v.shape[1]))


def scatter_ring(v, axis, pairs, me, count):
    rows = v.shape[0] // count
    got = [
        lax.ppermute(block_of(v, (me + s) % count, rows), axis, pairs(s)) for s in (2, 1, 3)
    ]
    return block_of(v, me, rows) + got[0] + got[1] + got[2]


def gather_ring(v, axis, pairs, me, count):
    rows = v.shape[0]
    out = jnp.zeros((rows * count, v.shape[1]), v.dtype)
    out = lax.dynamic_update_slice(out, v, (me * rows, 0))
    for s in (2, 1, 3):
        got = lax.ppermute(v, axis, pairs(s))
        out = lax.dynamic_update_slice(out, got, (((me - s) % count) * rows, 0))
    return out


def sum_everywhere(v, x, y, core):
    rows = v.shape[0] // NC
    v = block_of(v, core, rows) + lax.ppermute(block_of(v, 1 - core, rows), "dp", CORE_PAIRS)
    v = scatter_ring(v, "queue", x_pairs, x, NX)
    v = scatter_ring(v, "dp", y_pairs, y, NY)
    for m in (1, 2, 4):
        v = v + lax.ppermute(v, "queue", z_flip(m))
    v = gather_ring(v, "dp", y_pairs, y, NY)
    v = gather_ring(v, "queue", x_pairs, x, NX)
    other = lax.ppermute(v, "dp", CORE_PAIRS)
    return jnp.where(
        core == 0, jnp.concatenate([v, other], axis=0), jnp.concatenate([other, v], axis=0)
    )


def local(features, weight, support_queue, owner_shard, slot_row, loss_weight):
    n = features.shape[0]
    width = weight.shape[1]
    place = lax.axis_index("queue")
    x = place % NX
    group = lax.axis_index("dp")
    y, core = group // NC, group % NC

    wanted, places = plan(owner_shard, slot_row[:, None])
    asked = lax.all_to_all(wanted, "queue", split_axis=0, concat_axis=0, tiled=True)

    projected = jnp.dot(features, weight, preferred_element_type=F32)
    inv_norm = lax.rsqrt(jnp.sum(projected * projected, axis=1, keepdims=True) + EPSILON)
    unit_view = projected * inv_norm
    view_bf = unit_view.astype(BF)
    views = {0: view_bf}
    up = down = view_bf
    for d in (1, 2, 3):
        up = lax.ppermute(up, "queue", z_pairs(1))
        down = lax.ppermute(down, "queue", z_pairs(-1))
        views[NZ - d], views[d] = up, down
    views[4] = lax.ppermute(up, "queue", z_pairs(1))
    views = [views[d] for d in range(NZ)]

    picked = unit_rows(support_queue[asked].astype(F32)).astype(BF)
    answered = lax.all_to_all(picked, "queue", split_axis=0, concat_axis=0, tiled=True)
    anchors = answered.reshape(NZ * NX * CAP, width)[places[:, 0]]

    extra = jnp.zeros((16, width), BF).at[: n // width].set(loss_weight.reshape(n // width, width))
    message = jnp.concatenate([anchors, extra], axis=0)

    blocks = [message] + [lax.ppermute(message, "queue", x_pairs(k)) for k in (1, 2, 3)]
    parts, totals = {}, {}
    for b in (0, 1, 3, 2):
        parts[b], totals[b] = exps([blocks[b]], views)
    parts = [parts[b] for b in range(NX)]
    total = jnp.concatenate([totals[b] for b in range(NX)], axis=1)
    everyone = [total] + [lax.ppermute(total, "queue", x_pairs(k)) for k in (1, 2, 3)]
    scaled = scale(blocks, everyone, n)

    up = mix(scaled, parts, 4, BF)
    down = mix(scaled, parts, NZ - 3, BF)
    for d in (3, 2, 1):
        up = lax.ppermute(up, "queue", z_pairs(1)).astype(F32)
        up = (up + mix(scaled, parts, d, F32)).astype(BF)
        if d > 1:
            down = lax.ppermute(down, "queue", z_pairs(-1)).astype(F32)
            down = (down + mix(scaled, parts, NZ - d + 1, F32)).astype(BF)
    up = lax.ppermute(up, "queue", z_pairs(1)).astype(F32)
    down = lax.ppermute(down, "queue", z_pairs(-1)).astype(F32)
    own = mix(scaled, parts, 0, F32)
    weights = loss_weight.astype(F32)[:, None]
    grad_unit = own + up + down - (1.0 / TEMPER) * weights * anchors.astype(F32)

    grad_proj = (
        grad_unit - unit_view * jnp.sum(unit_view * grad_unit, axis=1, keepdims=True)
    ) * inv_norm
    grad_proj_bf = grad_proj.astype(BF)
    partial_weight = lax.dot_general(
        features, grad_proj_bf, (((0,), (0,)), ((), ())), preferred_element_type=F32
    )
    grad_feats = jnp.dot(grad_proj_bf, weight.T, preferred_element_type=F32).astype(BF)
    grad_weight = sum_everywhere(partial_weight, x, y, core)
    return (grad_feats, grad_weight)


def solution(mesh):
    in_specs = (
        P(("dp", "queue"), None),
        P(),
        P("queue", None),
        P(("dp", "queue"), None),
        P(("dp", "queue")),
        P(("dp", "queue")),
    )
    out_specs = (P(("dp", "queue"), None), P())
    return jax.shard_map(local, mesh=mesh, in_specs=in_specs, out_specs=out_specs, check_vma=False)
```

```python
import math

import jax
import jax.numpy as jnp
from jax import lax
from jax.experimental import pallas as pl
from jax.experimental.pallas import tpu as pltpu
from jax.sharding import Mesh
from jax.sharding import PartitionSpec as P

TEMPER = 0.1
EPSILON = 1e-06
NZ, NX, NY, NC = 8, 4, 4, 2
CAP = 64
BF = jnp.bfloat16
F32 = jnp.float32
VMEM_LIMIT = 48 * 1024 * 1024
EXPONENT = math.log2(math.e) / TEMPER
QUEUE = ("z", "x")


def shift(size, by):
    return [(i, (i + by) % size) for i in range(size)]


def flip(size, mask):
    return [(i, i ^ mask) for i in range(size)]


def vmem_call(kernel, out_shape, name, limit=VMEM_LIMIT, **kw):
    return pl.pallas_call(
        kernel,
        out_shape=out_shape,
        compiler_params=pltpu.CompilerParams(vmem_limit_bytes=limit),
        name=name,
        **kw,
    )


def plan_kernel(owner_ref, slot_ref, wanted_ref, places_ref):
    n = owner_ref.shape[0]
    owner = owner_ref[...]
    slot = slot_ref[...]
    shard = lax.broadcasted_iota(jnp.int32, (n, 128), 1)
    onehot = (owner == shard).astype(F32)
    below = (
        lax.broadcasted_iota(jnp.int32, (n, n), 1) < lax.broadcasted_iota(jnp.int32, (n, n), 0)
    ).astype(F32).astype(BF)
    before = jnp.dot(below, onehot.astype(BF), preferred_element_type=F32)
    rank = jnp.sum(before * onehot, axis=1, keepdims=True).astype(jnp.int32)
    places_ref[...] = owner * CAP + rank
    chosen = rank == lax.broadcasted_iota(jnp.int32, (n, 128), 1)
    high = jnp.where(chosen, (slot >> 7).astype(F32), 0.0).astype(BF)
    low = jnp.where(chosen, (slot & 127).astype(F32), 0.0).astype(BF)
    across = (((0,), (0,)), ((), ()))
    hot = onehot.astype(BF)
    upper = lax.dot_general(hot, high, across, preferred_element_type=F32)
    lower = lax.dot_general(hot, low, across, preferred_element_type=F32)
    full = upper.astype(jnp.int32) * 128 + lower.astype(jnp.int32)
    wanted_ref[...] = full[: wanted_ref.shape[0], :CAP]


def plan(owner, slot):
    n = owner.shape[0]
    return vmem_call(
        plan_kernel,
        (
            jax.ShapeDtypeStruct((NZ * NX, CAP), jnp.int32),
            jax.ShapeDtypeStruct((n, 1), jnp.int32),
        ),
        "plan",
    )(owner, slot)


def pick_kernel(rows_ref, places_ref, extra_ref, out_ref):
    n = places_ref.shape[0]
    places = places_ref[...]
    column = lax.broadcasted_iota(jnp.int32, (n, n), 1)
    total = None
    for at in range(0, rows_ref.shape[0], n):
        onehot = jnp.where(places == column + at, 1.0, 0.0).astype(BF)
        term = jnp.dot(onehot, rows_ref[at : at + n, :], preferred_element_type=F32)
        total = term if total is None else total + term
    unit = total * lax.rsqrt(jnp.sum(total * total, axis=1, keepdims=True) + EPSILON)
    out_ref[:n, :] = unit.astype(BF)
    out_ref[n:, :] = extra_ref[...]


def pick(rows, places, extra):
    n = places.shape[0]
    return vmem_call(
        pick_kernel, jax.ShapeDtypeStruct((n + extra.shape[0], rows.shape[1]), BF), "pick"
    )(rows, places, extra)


def exps_kernel(a_ref, v_ref, e_ref, t_ref, sum_ref):
    step = pl.program_id(0)
    n = e_ref.shape[2]
    a = a_ref[:n, :]
    half = v_ref.shape[1] // 2
    total = jnp.zeros((8, n), F32)
    for k in range(v_ref.shape[0]):
        for at in (0, half):
            dots = lax.dot_general(
                v_ref[k, at : at + half, :], a, (((1,), (1,)), ((), ())), preferred_element_type=F32
            )
            e = jnp.exp2(dots * EXPONENT)
            total = total + jnp.sum(e.reshape(half // 8, 8, n), axis=0)
            e_ref[k, at : at + half, :] = e.astype(BF)

    @pl.when(step == 0)
    def _():
        sum_ref[...] = total

    @pl.when(step > 0)
    def _():
        sum_ref[...] += total

    @pl.when(step == pl.num_programs(0) - 1)
    def _():
        t_ref[...] = jnp.sum(sum_ref[...], axis=0, keepdims=True)


def exps(anchors, views):
    many, n, width = views.shape
    each = 2
    return vmem_call(
        exps_kernel,
        (jax.ShapeDtypeStruct((many, n, n), BF), jax.ShapeDtypeStruct((1, n), F32)),
        "exps",
        grid=(many // each,),
        in_specs=[
            pl.BlockSpec(anchors.shape, lambda i: (0, 0)),
            pl.BlockSpec((each, n, width), lambda i: (i, 0, 0)),
        ],
        out_specs=(
            pl.BlockSpec((each, n, n), lambda i: (i, 0, 0)),
            pl.BlockSpec((1, n), lambda i: (0, 0)),
        ),
        scratch_shapes=[pltpu.VMEM((8, n), F32)],
    )(anchors, views)


def scale_kernel(*refs):
    anchors = refs[:NX]
    totals = refs[NX : 2 * NX]
    out_ref = refs[2 * NX]
    n = out_ref.shape[0] // NX
    width = out_ref.shape[1]
    for b in range(NX):
        t = None
        for k in range(NX):
            at = ((b - k) % NX) * n
            piece = totals[k][:, at : at + n]
            t = piece if t is None else t + piece
        w = anchors[b][n : n + 16, :].astype(F32)
        w = jnp.concatenate([w[k : k + 1, :] for k in range(n // width)], axis=1)
        c = (1.0 / TEMPER) * w / t
        column = jnp.broadcast_to(c, (8, n)).T[:, :1]
        out_ref[b * n : (b + 1) * n, :] = (anchors[b][:n, :].astype(F32) * column).astype(BF)


def scale(anchors, totals, n):
    return vmem_call(
        scale_kernel,
        jax.ShapeDtypeStruct((NX * n, anchors[0].shape[1]), BF),
        "scale",
    )(*anchors, *totals)


def product(a_ref, parts):
    total = None
    for b, part in enumerate(parts):
        size = part.shape[2]
        term = jnp.dot(part[0], a_ref[b * size : (b + 1) * size, :], preferred_element_type=F32)
        total = term if total is None else total + term
    return total


def first_kernel(order_ref, a_ref, *refs):
    value = product(a_ref, refs[:NX]).astype(BF)
    for i in range(2):

        @pl.when(pl.program_id(0) == i)
        def _():
            refs[NX + i][...] = value


def rest_kernel(order_ref, a_ref, *refs):
    refs[NX][0] = product(a_ref, refs[:NX])


def mix(kernel, order, scaled, parts, out_shape, out_specs, name):
    n = parts[0].shape[1]
    return vmem_call(
        kernel,
        out_shape,
        name,
        grid_spec=pltpu.PrefetchScalarGridSpec(
            num_scalar_prefetch=1,
            grid=order.shape,
            in_specs=[pl.BlockSpec(scaled.shape, lambda i, order: (0, 0))]
            + [pl.BlockSpec((1, n, p.shape[2]), lambda i, order: (order[i], 0, 0)) for p in parts],
            out_specs=out_specs,
        ),
    )(order, scaled, *parts)


def mix_first(order, scaled, parts):
    n, width = parts[0].shape[1], scaled.shape[1]
    one = jax.ShapeDtypeStruct((n, width), BF)
    spec = pl.BlockSpec((n, width), lambda i, order: (0, 0))
    return mix(first_kernel, order, scaled, parts, (one, one), (spec, spec), "mix_first")


def mix_rest(order, scaled, parts):
    n, width = parts[0].shape[1], scaled.shape[1]
    shape = jax.ShapeDtypeStruct(order.shape + (n, width), F32)
    spec = pl.BlockSpec((1, n, width), lambda i, order: (i, 0, 0))
    return mix(rest_kernel, order, scaled, parts, shape, spec, "mix_rest")


def finish_kernel(
    up_ref, down_ref, own_ref, anchors_ref, w_ref, unit_ref, inv_ref, feats_ref, grad_ref, part_ref
):
    n = up_ref.shape[0]
    unit = unit_ref[...]
    mixed = own_ref[0] + up_ref[...].astype(F32) + down_ref[...].astype(F32)
    grad = mixed - (1.0 / TEMPER) * w_ref[...] * anchors_ref[:n, :].astype(F32)
    along = jnp.sum(unit * grad, axis=1, keepdims=True)
    grad = ((grad - unit * along) * inv_ref[...]).astype(BF)
    grad_ref[...] = grad
    part_ref[...] = jnp.dot(feats_ref[...], grad, preferred_element_type=F32)


def finish(up, down, rest, anchors, w, unit, inv, feats_t):
    n, width = up.shape
    whole = lambda v: pl.BlockSpec(v.shape, lambda i: (0,) * v.ndim)
    last = rest.shape[0] - 1
    depth = feats_t.shape[0]
    return vmem_call(
        finish_kernel,
        (jax.ShapeDtypeStruct((n, width), BF), jax.ShapeDtypeStruct((depth, width), F32)),
        "finish",
        grid=(1,),
        in_specs=[
            whole(up),
            whole(down),
            pl.BlockSpec((1, n, width), lambda i: (last, 0, 0)),
            whole(anchors),
            whole(w),
            whole(unit),
            whole(inv),
            whole(feats_t),
        ],
        out_specs=(
            pl.BlockSpec((n, width), lambda i: (0, 0)),
            pl.BlockSpec((depth, width), lambda i: (0, 0)),
        ),
    )(up, down, rest, anchors, w, unit, inv, feats_t)


def block_of(v, index, rows):
    return lax.dynamic_slice(v, (index * rows, 0), (rows, v.shape[1]))


def sum_everywhere(v):
    width = v.shape[1]
    core = lax.axis_index("core")
    rows = v.shape[0] // NC
    v = block_of(v, core, rows) + lax.ppermute(block_of(v, 1 - core, rows), "core", flip(NC, 1))
    many = NY * NX
    v = lax.all_to_all(v, ("y", "x"), 0, 0, tiled=True)
    v = jnp.sum(v.reshape(many, rows // many, width), axis=0)
    got = [lax.ppermute(v, "z", flip(NZ, m)) for m in (1, 2, 3)]
    v = (v + got[0]) + (got[1] + got[2])
    v = v + lax.ppermute(v, "z", flip(NZ, 4))
    v = lax.optimization_barrier(jnp.broadcast_to(v[None], (many,) + v.shape))
    v = lax.all_to_all(v.reshape(rows, width), ("y", "x"), 0, 0, tiled=True)
    other = lax.ppermute(v, "core", flip(NC, 1))
    return jnp.where(
        core == 0, jnp.concatenate([v, other], axis=0), jnp.concatenate([other, v], axis=0)
    )


def local(features, weight, support_queue, owner_shard, slot_row, loss_weight):
    n = features.shape[0]
    width = weight.shape[1]
    z = lax.axis_index("z")

    wanted, places = plan(owner_shard, slot_row[:, None])
    asked = lax.all_to_all(wanted, QUEUE, split_axis=0, concat_axis=0, tiled=True)

    projected = jnp.dot(features, weight, preferred_element_type=F32)
    inv_norm = lax.rsqrt(jnp.sum(projected * projected, axis=1, keepdims=True) + EPSILON)
    unit_view = projected * inv_norm
    views = lax.all_gather(unit_view.astype(BF), "z", axis=0, tiled=False)
    feats_t = lax.optimization_barrier(features.T)

    picked = support_queue[asked]
    answered = lax.all_to_all(picked, QUEUE, split_axis=0, concat_axis=0, tiled=True)
    extra = jnp.zeros((16, width), BF).at[: n // width].set(loss_weight.reshape(n // width, width))
    message = pick(answered.reshape(NZ * NX * CAP, width), places, extra)

    blocks = [message] + [lax.ppermute(message, "x", shift(NX, k)) for k in (1, 2, 3)]
    parts, totals = {}, {}
    for b in (0, 1, 3, 2):
        parts[b], totals[b] = exps(blocks[b], views)
    parts = [parts[b] for b in range(NX)]
    total = jnp.concatenate([totals[b] for b in range(NX)], axis=1)
    everyone = [total] + [lax.ppermute(total, "x", shift(NX, k)) for k in (1, 2, 3)]
    scaled = scale(blocks, everyone, n)

    up, down = mix_first((z + jnp.array([4, 5], jnp.int32)) % NZ, scaled, parts)
    rest = mix_rest((z + jnp.array([3, 6, 2, 7, 1, 0], jnp.int32)) % NZ, scaled, parts)
    for k in range(3):
        up = lax.ppermute(up, "z", shift(NZ, 1)).astype(F32)
        up = (up + rest[2 * k]).astype(BF)
        if k < 2:
            down = lax.ppermute(down, "z", shift(NZ, -1)).astype(F32)
            down = (down + rest[2 * k + 1]).astype(BF)
    up = lax.ppermute(up, "z", shift(NZ, 1))
    down = lax.ppermute(down, "z", shift(NZ, -1))

    weights = loss_weight.astype(F32)[:, None]
    grad_proj, partial_weight = finish(
        up, down, rest, message, weights, unit_view, inv_norm, feats_t
    )
    grad_feats = jnp.dot(grad_proj, weight.T, preferred_element_type=F32).astype(BF)
    grad_weight = sum_everywhere(partial_weight)
    return (grad_feats, grad_weight)


def solution(mesh):
    mesh = Mesh(mesh.devices.reshape(NY, NC, NZ, NX), ("y", "core", "z", "x"))
    views = ("y", "core", "z", "x")
    in_specs = (
        P(views, None),
        P(),
        P(QUEUE, None),
        P(views, None),
        P(views),
        P(views),
    )
    out_specs = (P(views, None), P())
    return jax.shard_map(local, mesh=mesh, in_specs=in_specs, out_specs=out_specs, check_vma=False)
```

```python
import functools
import math

import jax
import jax.numpy as jnp
from jax import lax
from jax.experimental import pallas as pl
from jax.experimental.pallas import tpu as pltpu
from jax.sharding import Mesh
from jax.sharding import PartitionSpec as P

TEMPER = 0.1
EPSILON = 1e-06
NZ, NX, NY, NC = 8, 4, 4, 2
CAP = 64
BF = jnp.bfloat16
F32 = jnp.float32
VMEM_LIMIT = 16 * 1024 * 1024
IN_VMEM = pl.BlockSpec(memory_space=pltpu.VMEM)
EXPONENT = math.log2(math.e) / TEMPER
QUEUE = ("z", "x")


def shift(size, by):
    return [(i, (i + by) % size) for i in range(size)]


def flip(size, mask):
    return [(i, i ^ mask) for i in range(size)]


def vmem_call(kernel, out_shape, name, limit=VMEM_LIMIT, **kw):
    return pl.pallas_call(
        kernel,
        out_shape=out_shape,
        compiler_params=pltpu.CompilerParams(vmem_limit_bytes=limit),
        name=name,
        **kw,
    )


def begin_kernel(
    feats_ref, weight_ref, owner_ref, slot_ref, unit_ref, inv_ref, view_ref, wanted_ref, places_ref
):
    n = feats_ref.shape[0]
    shards = wanted_ref.shape[0]
    owner = owner_ref[...]
    slot = slot_ref[...]
    onehot = jnp.where(owner == lax.broadcasted_iota(jnp.int32, (shards, n), 0), 1.0, 0.0)
    above = lax.broadcasted_iota(jnp.int32, (n, n), 0) < lax.broadcasted_iota(jnp.int32, (n, n), 1)
    above = jnp.where(above, 1.0, 0.0).astype(BF)
    before = jnp.dot(onehot.astype(BF), above, preferred_element_type=F32)
    rank = jnp.sum(before * onehot, axis=0, keepdims=True).astype(jnp.int32)
    chosen = jnp.where(rank == lax.broadcasted_iota(jnp.int32, (128, n), 0), 1.0, 0.0).astype(BF)
    both = (((1,), (1,)), ((), ()))
    high = (onehot * (slot >> 7).astype(F32)).astype(BF)
    low = (onehot * (slot & 127).astype(F32)).astype(BF)
    upper = lax.dot_general(high, chosen, both, preferred_element_type=F32)
    lower = lax.dot_general(low, chosen, both, preferred_element_type=F32)
    full = upper.astype(jnp.int32) * 128 + lower.astype(jnp.int32)
    wanted_ref[...] = full[:, :CAP]
    places_ref[...] = jnp.broadcast_to(owner * CAP + rank, (8, n)).T[:, :1]

    projected = jnp.dot(feats_ref[...], weight_ref[...], preferred_element_type=F32)
    inv = lax.rsqrt(jnp.sum(projected * projected, axis=1, keepdims=True) + EPSILON)
    unit = projected * inv
    inv_ref[...] = inv
    unit_ref[...] = unit
    view_ref[...] = unit.astype(BF)


def begin(features, weight, owner, slot):
    n, width = features.shape[0], weight.shape[1]
    return vmem_call(
        begin_kernel,
        (
            jax.ShapeDtypeStruct((n, width), F32),
            jax.ShapeDtypeStruct((n, 1), F32),
            jax.ShapeDtypeStruct((n, width), BF),
            jax.ShapeDtypeStruct((NZ * NX, CAP), jnp.int32),
            jax.ShapeDtypeStruct((n, 1), jnp.int32),
        ),
        "begin",
    )(features, weight, owner, slot)


def pick_kernel(rows_ref, places_ref, extra_ref, out_ref):
    n = places_ref.shape[0]
    places = places_ref[...]
    column = lax.broadcasted_iota(jnp.int32, (n, n), 1)
    total = None
    for at in range(0, rows_ref.shape[0], n):
        onehot = jnp.where(places == column + at, 1.0, 0.0).astype(BF)
        term = jnp.dot(onehot, rows_ref[at : at + n, :], preferred_element_type=F32)
        total = term if total is None else total + term
    unit = total * lax.rsqrt(jnp.sum(total * total, axis=1, keepdims=True) + EPSILON)
    out_ref[:n, :] = unit.astype(BF)
    out_ref[n:, :] = extra_ref[...]


def pick(rows, places, extra):
    n = places.shape[0]
    return vmem_call(
        pick_kernel, jax.ShapeDtypeStruct((n + extra.shape[0], rows.shape[1]), BF), "pick"
    )(rows, places, extra)


def exps_kernel(a_ref, *refs):
    views, (e_ref, t_ref) = refs[:NZ], refs[NZ:]
    n = t_ref.shape[1]
    a = a_ref[:n, :]
    total = jnp.zeros((8, n), F32)
    for k in range(NZ):
        dots = lax.dot_general(
            views[k][...], a, (((1,), (1,)), ((), ())), preferred_element_type=F32
        )
        e = jnp.exp2(dots * EXPONENT)
        total = total + jnp.sum(e.reshape(n // 8, 8, n), axis=0)
        e_ref[k] = e.astype(BF)
    t_ref[...] = jnp.sum(total, axis=0, keepdims=True)


def exps(anchors, views):
    n = views[0].shape[0]
    return vmem_call(
        exps_kernel,
        (jax.ShapeDtypeStruct((NZ, n, n), BF), jax.ShapeDtypeStruct((1, n), F32)),
        "exps",
        in_specs=[IN_VMEM] * (1 + NZ),
        out_specs=(IN_VMEM, IN_VMEM),
    )(anchors, *views)


def scale_kernel(*refs):
    anchors = refs[:NX]
    totals = refs[NX : 2 * NX]
    out_ref = refs[2 * NX]
    n = out_ref.shape[0] // NX
    width = out_ref.shape[1]
    for b in range(NX):
        t = None
        for k in range(NX):
            at = ((b - k) % NX) * n
            piece = totals[k][:, at : at + n]
            t = piece if t is None else t + piece
        w = anchors[b][n : n + 16, :].astype(F32)
        w = jnp.concatenate([w[k : k + 1, :] for k in range(n // width)], axis=1)
        c = (1.0 / TEMPER) * w / t
        column = jnp.broadcast_to(c, (8, n)).T[:, :1]
        out_ref[b * n : (b + 1) * n, :] = (anchors[b][:n, :].astype(F32) * column).astype(BF)


def scale(anchors, totals, n):
    return vmem_call(
        scale_kernel,
        jax.ShapeDtypeStruct((NX * n, anchors[0].shape[1]), BF),
        "scale",
    )(*anchors, *totals)


def mix_kernel(which, a_ref, *refs):
    parts, outs = refs[:NX], refs[NX:]
    for k, out in zip(which, outs):
        total = None
        for b, part in enumerate(parts):
            size = part.shape[2]
            term = jnp.dot(part[k], a_ref[b * size : (b + 1) * size, :], preferred_element_type=F32)
            total = term if total is None else total + term
        out[...] = total.astype(out.dtype)


def mix(which, scaled, parts, dtype):
    shape = jax.ShapeDtypeStruct((parts[0].shape[1], scaled.shape[1]), dtype)
    return vmem_call(
        functools.partial(mix_kernel, which),
        tuple(shape for _ in which),
        "mix",
        in_specs=[IN_VMEM] * (1 + NX),
        out_specs=tuple(IN_VMEM for _ in which),
    )(scaled, *parts)


def finish_kernel(
    up_ref, down_ref, own_ref, anchors_ref, w_ref, unit_ref, inv_ref, feats_ref, grad_ref, part_ref
):
    n = up_ref.shape[0]
    unit = unit_ref[...]
    mixed = own_ref[...] + up_ref[...].astype(F32) + down_ref[...].astype(F32)
    grad = mixed - (1.0 / TEMPER) * w_ref[...] * anchors_ref[:n, :].astype(F32)
    along = jnp.sum(unit * grad, axis=1, keepdims=True)
    grad = ((grad - unit * along) * inv_ref[...]).astype(BF)
    grad_ref[...] = grad
    part_ref[...] = jnp.dot(feats_ref[...], grad, preferred_element_type=F32)


def finish(up, down, own, anchors, w, unit, inv, feats_t):
    n, width = up.shape
    return vmem_call(
        finish_kernel,
        (
            jax.ShapeDtypeStruct((n, width), BF),
            jax.ShapeDtypeStruct((feats_t.shape[0], width), F32),
        ),
        "finish",
    )(up, down, own, anchors, w, unit, inv, feats_t)


def block_of(v, index, rows):
    return lax.dynamic_slice(v, (index * rows, 0), (rows, v.shape[1]))


def sum_everywhere(v):
    width = v.shape[1]
    core = lax.axis_index("core")
    rows = v.shape[0] // NC
    v = block_of(v, core, rows) + lax.ppermute(block_of(v, 1 - core, rows), "core", flip(NC, 1))
    many = NY * NX
    v = lax.all_to_all(v, ("y", "x"), 0, 0, tiled=True)
    v = jnp.sum(v.reshape(many, rows // many, width), axis=0)
    got = [lax.ppermute(v, "z", flip(NZ, m)) for m in (1, 2, 3)]
    v = (v + got[0]) + (got[1] + got[2])
    v = v + lax.ppermute(v, "z", flip(NZ, 4))
    v = lax.optimization_barrier(jnp.broadcast_to(v[None], (many,) + v.shape))
    v = lax.all_to_all(v.reshape(rows, width), ("y", "x"), 0, 0, tiled=True)
    other = lax.ppermute(v, "core", flip(NC, 1))
    return jnp.where(
        core == 0, jnp.concatenate([v, other], axis=0), jnp.concatenate([other, v], axis=0)
    )


def local(features, weight, support_queue, owner_shard, slot_row, loss_weight):
    n = features.shape[0]
    width = weight.shape[1]

    unit_view, inv_norm, view_bf, wanted, places = begin(
        features, weight, owner_shard.reshape(1, n), slot_row.reshape(1, n)
    )
    views = {0: view_bf}
    views[7] = lax.ppermute(view_bf, "z", shift(NZ, 1))
    views[1] = lax.ppermute(view_bf, "z", shift(NZ, -1))
    asked = lax.all_to_all(wanted, QUEUE, split_axis=0, concat_axis=0, tiled=True)
    asked, views[7], views[1] = lax.optimization_barrier((asked, views[7], views[1]))
    views[6] = lax.ppermute(views[7], "z", shift(NZ, 1))
    views[2] = lax.ppermute(views[1], "z", shift(NZ, -1))
    picked = support_queue[asked]
    picked, views[6], views[2] = lax.optimization_barrier((picked, views[6], views[2]))
    views[5] = lax.ppermute(views[6], "z", shift(NZ, 1))
    views[3] = lax.ppermute(views[2], "z", shift(NZ, -1))
    views[4] = lax.ppermute(views[5], "z", shift(NZ, 1))
    views = [views[d] for d in range(NZ)]
    feats_t = lax.optimization_barrier(features.T)

    answered = lax.all_to_all(picked, QUEUE, split_axis=0, concat_axis=0, tiled=True)
    extra = jnp.zeros((16, width), BF).at[: n // width].set(loss_weight.reshape(n // width, width))
    message = pick(answered.reshape(NZ * NX * CAP, width), places, extra)

    blocks = [message] + [lax.ppermute(message, "x", shift(NX, k)) for k in (1, 2, 3)]
    parts, totals = {}, {}
    for b in (0, 1, 3, 2):
        parts[b], totals[b] = exps(blocks[b], views)
    parts = [parts[b] for b in range(NX)]
    total = jnp.concatenate([totals[b] for b in range(NX)], axis=1)
    everyone = [total] + [lax.ppermute(total, "x", shift(NX, k)) for k in (1, 2, 3)]
    scaled = scale(blocks, everyone, n)

    up, down = mix((4, 5), scaled, parts, BF)
    for ahead, behind in ((3, 6), (2, 7), (1, 0)):
        up_part, down_part = mix((ahead, behind), scaled, parts, F32)
        up = (lax.ppermute(up, "z", shift(NZ, 1)).astype(F32) + up_part).astype(BF)
        if behind:
            down = (lax.ppermute(down, "z", shift(NZ, -1)).astype(F32) + down_part).astype(BF)
    up = lax.ppermute(up, "z", shift(NZ, 1))
    down = lax.ppermute(down, "z", shift(NZ, -1))

    weights = loss_weight.astype(F32)[:, None]
    grad_proj, partial_weight = finish(
        up, down, down_part, message, weights, unit_view, inv_norm, feats_t
    )
    grad_feats = jnp.dot(grad_proj, weight.T, preferred_element_type=F32).astype(BF)
    grad_weight = sum_everywhere(partial_weight)
    return (grad_feats, grad_weight)


def solution(mesh):
    mesh = Mesh(mesh.devices.reshape(NY, NC, NZ, NX), ("y", "core", "z", "x"))
    views = ("y", "core", "z", "x")
    in_specs = (
        P(views, None),
        P(),
        P(QUEUE, None),
        P(views, None),
        P(views),
        P(views),
    )
    out_specs = (P(views, None), P())
    return jax.shard_map(local, mesh=mesh, in_specs=in_specs, out_specs=out_specs, check_vma=False)
```

```python
import functools
import math

import jax
import jax.numpy as jnp
from jax import lax
from jax.experimental import pallas as pl
from jax.experimental.pallas import tpu as pltpu
from jax.sharding import Mesh
from jax.sharding import PartitionSpec as P

TEMPER = 0.1
EPSILON = 1e-06
NZ, NX, NY, NC = 8, 4, 4, 2
CAP = 64
BF = jnp.bfloat16
F32 = jnp.float32
VMEM_LIMIT = 16 * 1024 * 1024
ALL_VMEM = 62 * 1024 * 1024
IN_VMEM = pl.BlockSpec(memory_space=pltpu.VMEM)
EXPONENT = math.log2(math.e) / TEMPER
QUEUE = ("z", "x")


def shift(size, by):
    return [(i, (i + by) % size) for i in range(size)]


def flip(size, mask):
    return [(i, i ^ mask) for i in range(size)]


def vmem_call(kernel, out_shape, name, limit=VMEM_LIMIT, **kw):
    return pl.pallas_call(
        kernel,
        out_shape=out_shape,
        compiler_params=pltpu.CompilerParams(vmem_limit_bytes=limit),
        name=name,
        **kw,
    )


def ranks(owner, shards):
    n = owner.shape[1]
    onehot = jnp.where(owner == lax.broadcasted_iota(jnp.int32, (shards, n), 0), 1.0, 0.0)
    above = lax.broadcasted_iota(jnp.int32, (n, n), 0) < lax.broadcasted_iota(jnp.int32, (n, n), 1)
    above = jnp.where(above, 1.0, 0.0).astype(BF)
    before = jnp.dot(onehot.astype(BF), above, preferred_element_type=F32)
    return onehot, jnp.sum(before * onehot, axis=0, keepdims=True).astype(jnp.int32)


def project(features, weight):
    projected = jnp.dot(features, weight, preferred_element_type=F32)
    inv = lax.rsqrt(jnp.sum(projected * projected, axis=1, keepdims=True) + EPSILON)
    return projected * inv, inv


def begin_kernel(
    feats_hbm,
    weight_hbm,
    owner_hbm,
    slot_hbm,
    view_ref,
    wanted_ref,
    feats_ref,
    weight_ref,
    owner_ref,
    slot_ref,
    sems,
):
    copies = [
        pltpu.make_async_copy(owner_hbm, owner_ref, sems.at[0]),
        pltpu.make_async_copy(slot_hbm, slot_ref, sems.at[1]),
        pltpu.make_async_copy(weight_hbm, weight_ref, sems.at[2]),
        pltpu.make_async_copy(feats_hbm, feats_ref, sems.at[3]),
    ]
    for copy in copies:
        copy.start()
    copies[0].wait()
    copies[1].wait()
    n = owner_ref.shape[1]
    slot = slot_ref[...]
    onehot, rank = ranks(owner_ref[...], wanted_ref.shape[0])
    chosen = jnp.where(rank == lax.broadcasted_iota(jnp.int32, (128, n), 0), 1.0, 0.0).astype(BF)
    both = (((1,), (1,)), ((), ()))
    high = (onehot * (slot >> 7).astype(F32)).astype(BF)
    low = (onehot * (slot & 127).astype(F32)).astype(BF)
    upper = lax.dot_general(high, chosen, both, preferred_element_type=F32)
    lower = lax.dot_general(low, chosen, both, preferred_element_type=F32)
    full = upper.astype(jnp.int32) * 128 + lower.astype(jnp.int32)
    wanted_ref[...] = full[:, :CAP]
    copies[2].wait()
    copies[3].wait()
    view_ref[...] = project(feats_ref[...], weight_ref[...])[0].astype(BF)


def begin(features, weight, owner, slot):
    n, width = features.shape[0], weight.shape[1]
    in_hbm = pl.BlockSpec(memory_space=pltpu.HBM)
    return vmem_call(
        begin_kernel,
        (
            jax.ShapeDtypeStruct((n, width), BF),
            jax.ShapeDtypeStruct((NZ * NX, CAP), jnp.int32),
        ),
        "begin",
        ALL_VMEM,
        in_specs=[in_hbm] * 4,
        out_specs=(IN_VMEM, IN_VMEM),
        scratch_shapes=[
            pltpu.VMEM(features.shape, BF),
            pltpu.VMEM(weight.shape, BF),
            pltpu.VMEM(owner.shape, jnp.int32),
            pltpu.VMEM(slot.shape, jnp.int32),
            pltpu.SemaphoreType.DMA((4,)),
        ],
    )(features, weight, owner, slot)


def column_of(row):
    return jnp.broadcast_to(row, (8, row.shape[1])).T[:, :1]


def pick_kernel(rows_ref, owner_ref, extra_ref, out_ref):
    n = owner_ref.shape[1]
    owner = owner_ref[...]
    places = column_of(owner * CAP + ranks(owner, rows_ref.shape[0] // CAP)[1])
    column = lax.broadcasted_iota(jnp.int32, (n, n), 1)
    total = None
    for at in range(0, rows_ref.shape[0], n):
        onehot = jnp.where(places == column + at, 1.0, 0.0).astype(BF)
        term = jnp.dot(onehot, rows_ref[at : at + n, :], preferred_element_type=F32)
        total = term if total is None else total + term
    unit = total * lax.rsqrt(jnp.sum(total * total, axis=1, keepdims=True) + EPSILON)
    out_ref[:n, :] = unit.astype(BF)
    out_ref[n:, :] = extra_ref[...]


def pick(rows, owner, extra):
    n = owner.shape[1]
    return vmem_call(
        pick_kernel,
        jax.ShapeDtypeStruct((n + extra.shape[0], rows.shape[1]), BF),
        "pick",
        in_specs=[IN_VMEM] * 3,
        out_specs=IN_VMEM,
    )(rows, owner, extra)


def exps_kernel(a_ref, *refs):
    views, (e_ref, t_ref) = refs[:NZ], refs[NZ:]
    n = t_ref.shape[1]
    a = a_ref[:n, :]
    total = jnp.zeros((8, n), F32)
    for k in range(NZ):
        dots = lax.dot_general(
            views[k][...], a, (((1,), (1,)), ((), ())), preferred_element_type=F32
        )
        e = jnp.exp2(dots * EXPONENT)
        total = total + jnp.sum(e.reshape(n // 8, 8, n), axis=0)
        e_ref[k] = e.astype(BF)
    t_ref[...] = jnp.sum(total, axis=0, keepdims=True)


def exps(anchors, views):
    n = views[0].shape[0]
    return vmem_call(
        exps_kernel,
        (jax.ShapeDtypeStruct((NZ, n, n), BF), jax.ShapeDtypeStruct((1, n), F32)),
        "exps",
        in_specs=[IN_VMEM] * (1 + NZ),
        out_specs=(IN_VMEM, IN_VMEM),
    )(anchors, *views)


def weights_of(message_ref, n):
    w = message_ref[n : n + 16, :].astype(F32)
    return jnp.concatenate([w[k : k + 1, :] for k in range(n // w.shape[1])], axis=1)


def scale_kernel(*refs):
    anchors = refs[:NX]
    totals = refs[NX : 2 * NX]
    out_ref = refs[2 * NX]
    n = out_ref.shape[0] // NX
    for b in range(NX):
        t = None
        for k in range(NX):
            at = ((b - k) % NX) * n
            piece = totals[k][:, at : at + n]
            t = piece if t is None else t + piece
        column = column_of((1.0 / TEMPER) * weights_of(anchors[b], n) / t)
        out_ref[b * n : (b + 1) * n, :] = (anchors[b][:n, :].astype(F32) * column).astype(BF)


def scale(anchors, totals, n):
    return vmem_call(
        scale_kernel,
        jax.ShapeDtypeStruct((NX * n, anchors[0].shape[1]), BF),
        "scale",
        in_specs=[IN_VMEM] * (2 * NX),
        out_specs=IN_VMEM,
    )(*anchors, *totals)


def mix_kernel(which, a_ref, *refs):
    parts, outs = refs[:NX], refs[NX:]
    for k, out in zip(which, outs):
        total = None
        for b, part in enumerate(parts):
            size = part.shape[2]
            term = jnp.dot(part[k], a_ref[b * size : (b + 1) * size, :], preferred_element_type=F32)
            total = term if total is None else total + term
        out[...] = total.astype(out.dtype)


def mix(which, scaled, parts, dtype):
    shape = jax.ShapeDtypeStruct((parts[0].shape[1], scaled.shape[1]), dtype)
    return vmem_call(
        functools.partial(mix_kernel, which),
        tuple(shape for _ in which),
        "mix",
        in_specs=[IN_VMEM] * (1 + NX),
        out_specs=tuple(IN_VMEM for _ in which),
    )(scaled, *parts)


def finish_kernel(
    core_ref,
    up_ref,
    down_ref,
    own_ref,
    message_ref,
    feats_ref,
    weight_ref,
    grad_ref,
    keep_ref,
    send_ref,
):
    n = up_ref.shape[0]
    feats = feats_ref[...]
    unit, inv = project(feats, weight_ref[...])
    mixed = own_ref[...] + up_ref[...].astype(F32) + down_ref[...].astype(F32)
    w = column_of((1.0 / TEMPER) * weights_of(message_ref, n))
    grad = mixed - w * message_ref[:n, :].astype(F32)
    along = jnp.sum(unit * grad, axis=1, keepdims=True)
    grad = ((grad - unit * along) * inv).astype(BF)
    grad_ref[...] = grad
    part = lax.dot_general(feats, grad, (((0,), (0,)), ((), ())), preferred_element_type=F32)
    half = keep_ref.shape[0]
    for core in range(NC):

        @pl.when(core_ref[0] == core)
        def _():
            keep_ref[...] = part[core * half : (core + 1) * half]
            send_ref[...] = part[(1 - core) * half : (2 - core) * half]


def finish(core, up, down, own, message, features, weight):
    n, width = up.shape
    half = jax.ShapeDtypeStruct((features.shape[1] // NC, width), F32)
    return vmem_call(
        finish_kernel,
        (jax.ShapeDtypeStruct((n, width), BF), half, half),
        "finish",
        in_specs=[pl.BlockSpec(memory_space=pltpu.SMEM)] + [IN_VMEM] * 6,
        out_specs=(IN_VMEM,) * 3,
    )(core.reshape(1), up, down, own, message, features, weight)


def sum_everywhere(keep, send, core, beside):
    rows, width = keep.shape
    v = keep + lax.ppermute(send, "core", flip(NC, 1))
    many = NY * NX
    v = lax.all_to_all(v, ("y", "x"), 0, 0, tiled=True)
    v = jnp.sum(v.reshape(many, rows // many, width), axis=0)
    got = [lax.ppermute(v, "z", flip(NZ, m)) for m in (1, 2, 3)]
    v = (v + got[0]) + (got[1] + got[2])
    v = v + lax.ppermute(v, "z", flip(NZ, 4))
    v, beside = lax.optimization_barrier((v, beside))
    v = lax.optimization_barrier(jnp.broadcast_to(v[None], (many,) + v.shape))
    v = lax.all_to_all(v.reshape(rows, width), ("y", "x"), 0, 0, tiled=True)
    other = lax.ppermute(v, "core", flip(NC, 1))
    low, high = jnp.where(core == 0, v, other), jnp.where(core == 0, other, v)
    return jnp.concatenate([low, high], axis=0), beside


def local(features, weight, support_queue, owner_shard, slot_row, loss_weight):
    n = features.shape[0]
    width = weight.shape[1]

    core = lax.axis_index("core")
    owner = owner_shard.reshape(1, n)
    view_bf, wanted = begin(features, weight, owner, slot_row.reshape(1, n))
    views = {0: view_bf}
    views[7] = lax.ppermute(view_bf, "z", shift(NZ, 1))
    views[1] = lax.ppermute(view_bf, "z", shift(NZ, -1))
    asked = lax.all_to_all(wanted, QUEUE, split_axis=0, concat_axis=0, tiled=True)
    asked, views[7], views[1] = lax.optimization_barrier((asked, views[7], views[1]))
    views[6] = lax.ppermute(views[7], "z", shift(NZ, 1))
    views[2] = lax.ppermute(views[1], "z", shift(NZ, -1))
    picked = support_queue[asked]
    picked, views[6], views[2] = lax.optimization_barrier((picked, views[6], views[2]))
    views[5] = lax.ppermute(views[6], "z", shift(NZ, 1))
    views[3] = lax.ppermute(views[2], "z", shift(NZ, -1))
    views[4] = lax.ppermute(views[5], "z", shift(NZ, 1))
    views = [views[d] for d in range(NZ)]

    answered = lax.all_to_all(picked, QUEUE, split_axis=0, concat_axis=0, tiled=True)
    extra = jnp.zeros((16, width), BF).at[: n // width].set(loss_weight.reshape(n // width, width))
    message = pick(answered.reshape(NZ * NX * CAP, width), owner, extra)

    blocks = [message] + [lax.ppermute(message, "x", shift(NX, k)) for k in (1, 2, 3)]
    parts, totals = {}, {}
    for b in (0, 1, 3, 2):
        parts[b], totals[b] = exps(blocks[b], views)
    parts = [parts[b] for b in range(NX)]
    total = jnp.concatenate([totals[b] for b in range(NX)], axis=1)
    everyone = [total] + [lax.ppermute(total, "x", shift(NX, k)) for k in (1, 2, 3)]
    scaled = scale(blocks, everyone, n)

    (far,) = mix((4,), scaled, parts, BF)
    up, down = far[: n // 2], far[n // 2 :]
    for d in (3, 2, 1):
        up_part, down_part = mix((d, NZ - d), scaled, parts, F32)
        up = lax.ppermute(up, "z", shift(NZ, 1)).astype(F32)
        down = lax.ppermute(down, "z", shift(NZ, -1)).astype(F32)
        if d == 3:
            up = jnp.concatenate([up + up_part[: n // 2], up_part[n // 2 :]], axis=0)
            down = jnp.concatenate([down_part[: n // 2], down + down_part[n // 2 :]], axis=0)
        else:
            up, down = up + up_part, down + down_part
        up, down = up.astype(BF), down.astype(BF)
    (own,) = mix((0,), scaled, parts, F32)
    up = lax.ppermute(up, "z", shift(NZ, 1))
    down = lax.ppermute(down, "z", shift(NZ, -1))

    grad_proj, keep, send = finish(core, up, down, own, message, features, weight)
    grad_feats = jnp.dot(grad_proj, weight.T, preferred_element_type=F32).astype(BF)
    grad_weight, grad_feats = sum_everywhere(keep, send, core, grad_feats)
    return (grad_feats, grad_weight)


def solution(mesh):
    mesh = Mesh(mesh.devices.reshape(NY, NC, NZ, NX), ("y", "core", "z", "x"))
    views = ("y", "core", "z", "x")
    in_specs = (
        P(views, None),
        P(),
        P(QUEUE, None),
        P(views, None),
        P(views),
        P(views),
    )
    out_specs = (P(views, None), P())
    return jax.shard_map(local, mesh=mesh, in_specs=in_specs, out_specs=out_specs, check_vma=False)
```

```python
import functools
import math

import jax
import jax.numpy as jnp
from jax import lax
from jax.experimental import pallas as pl
from jax.experimental.pallas import tpu as pltpu
from jax.sharding import Mesh
from jax.sharding import PartitionSpec as P

TEMPER = 0.1
EPSILON = 1e-06
NZ, NX, NY, NC = 8, 4, 4, 2
CAP = 64
BF = jnp.bfloat16
F32 = jnp.float32
VMEM_LIMIT = 16 * 1024 * 1024
ALL_VMEM = 62 * 1024 * 1024
IN_VMEM = pl.BlockSpec(memory_space=pltpu.VMEM)
EXPONENT = math.log2(math.e) / TEMPER
QUEUE = ("z", "x")


def shift(size, by):
    return [(i, (i + by) % size) for i in range(size)]


def flip(size, mask):
    return [(i, i ^ mask) for i in range(size)]


def vmem_call(kernel, out_shape, name, limit=VMEM_LIMIT, **kw):
    return pl.pallas_call(
        kernel,
        out_shape=out_shape,
        compiler_params=pltpu.CompilerParams(vmem_limit_bytes=limit),
        name=name,
        **kw,
    )


def ranks(owner, shards):
    n = owner.shape[1]
    onehot = jnp.where(owner == lax.broadcasted_iota(jnp.int32, (shards, n), 0), 1.0, 0.0)
    above = lax.broadcasted_iota(jnp.int32, (n, n), 0) < lax.broadcasted_iota(jnp.int32, (n, n), 1)
    above = jnp.where(above, 1.0, 0.0).astype(BF)
    before = jnp.dot(onehot.astype(BF), above, preferred_element_type=F32)
    return onehot, jnp.sum(before * onehot, axis=0, keepdims=True).astype(jnp.int32)


def project(features, weight):
    projected = jnp.dot(features, weight, preferred_element_type=F32)
    inv = lax.rsqrt(jnp.sum(projected * projected, axis=1, keepdims=True) + EPSILON)
    return projected * inv, inv


def begin_kernel(
    feats_hbm,
    weight_hbm,
    owner_hbm,
    slot_hbm,
    view_ref,
    wanted_ref,
    feats_ref,
    weight_ref,
    owner_ref,
    slot_ref,
    sems,
):
    copies = [
        pltpu.make_async_copy(owner_hbm, owner_ref, sems.at[0]),
        pltpu.make_async_copy(slot_hbm, slot_ref, sems.at[1]),
        pltpu.make_async_copy(weight_hbm, weight_ref, sems.at[2]),
        pltpu.make_async_copy(feats_hbm, feats_ref, sems.at[3]),
    ]
    for copy in copies:
        copy.start()
    copies[0].wait()
    copies[1].wait()
    n = owner_ref.shape[1]
    slot = slot_ref[...]
    onehot, rank = ranks(owner_ref[...], wanted_ref.shape[0])
    chosen = jnp.where(rank == lax.broadcasted_iota(jnp.int32, (128, n), 0), 1.0, 0.0).astype(BF)
    both = (((1,), (1,)), ((), ()))
    high = (onehot * (slot >> 7).astype(F32)).astype(BF)
    low = (onehot * (slot & 127).astype(F32)).astype(BF)
    upper = lax.dot_general(high, chosen, both, preferred_element_type=F32)
    lower = lax.dot_general(low, chosen, both, preferred_element_type=F32)
    full = upper.astype(jnp.int32) * 128 + lower.astype(jnp.int32)
    wanted_ref[...] = full[:, :CAP]
    copies[2].wait()
    copies[3].wait()
    view_ref[...] = project(feats_ref[...], weight_ref[...])[0].astype(BF)


def begin(features, weight, owner, slot):
    n, width = features.shape[0], weight.shape[1]
    in_hbm = pl.BlockSpec(memory_space=pltpu.HBM)
    return vmem_call(
        begin_kernel,
        (
            jax.ShapeDtypeStruct((n, width), BF),
            jax.ShapeDtypeStruct((NZ * NX, CAP), jnp.int32),
        ),
        "begin",
        ALL_VMEM,
        in_specs=[in_hbm] * 4,
        out_specs=(IN_VMEM, IN_VMEM),
        scratch_shapes=[
            pltpu.VMEM(features.shape, BF),
            pltpu.VMEM(weight.shape, BF),
            pltpu.VMEM(owner.shape, jnp.int32),
            pltpu.VMEM(slot.shape, jnp.int32),
            pltpu.SemaphoreType.DMA((4,)),
        ],
    )(features, weight, owner, slot)


def column_of(row):
    return jnp.broadcast_to(row, (8, row.shape[1])).T[:, :1]


def pick_kernel(first_ref, second_ref, owner_ref, extra_ref, out_ref):
    n = owner_ref.shape[1]
    half = CAP // 2
    slots = first_ref.shape[0]
    owner = owner_ref[...]
    rank = ranks(owner, slots // half)[1]
    late = rank >= half
    places = owner * half + jnp.where(late, slots + rank - half, rank)
    places = column_of(places)
    column = lax.broadcasted_iota(jnp.int32, (n, n), 1)
    total = None
    for k, rows_ref in enumerate((first_ref, second_ref)):
        for at in range(0, slots, n):
            onehot = jnp.where(places == column + (k * slots + at), 1.0, 0.0).astype(BF)
            term = jnp.dot(onehot, rows_ref[at : at + n, :], preferred_element_type=F32)
            total = term if total is None else total + term
    unit = total * lax.rsqrt(jnp.sum(total * total, axis=1, keepdims=True) + EPSILON)
    out_ref[:n, :] = unit.astype(BF)
    out_ref[n:, :] = extra_ref[...]


def pick(first, second, owner, extra):
    n = owner.shape[1]
    return vmem_call(
        pick_kernel,
        jax.ShapeDtypeStruct((n + extra.shape[0], first.shape[1]), BF),
        "pick",
        in_specs=[IN_VMEM] * 4,
        out_specs=IN_VMEM,
    )(first, second, owner, extra)


def exps_kernel(a_ref, *refs):
    views, (e_ref, t_ref) = refs[:NZ], refs[NZ:]
    n = t_ref.shape[1]
    a = a_ref[:n, :]
    total = jnp.zeros((8, n), F32)
    for k in range(NZ):
        dots = lax.dot_general(
            views[k][...], a, (((1,), (1,)), ((), ())), preferred_element_type=F32
        )
        e = jnp.exp2(dots * EXPONENT)
        total = total + jnp.sum(e.reshape(n // 8, 8, n), axis=0)
        e_ref[k] = e.astype(BF)
    t_ref[...] = jnp.sum(total, axis=0, keepdims=True)


def exps(anchors, views):
    n = views[0].shape[0]
    return vmem_call(
        exps_kernel,
        (jax.ShapeDtypeStruct((NZ, n, n), BF), jax.ShapeDtypeStruct((1, n), F32)),
        "exps",
        in_specs=[IN_VMEM] * (1 + NZ),
        out_specs=(IN_VMEM, IN_VMEM),
    )(anchors, *views)


def weights_of(message_ref, n):
    w = message_ref[n : n + 16, :].astype(F32)
    return jnp.concatenate([w[k : k + 1, :] for k in range(n // w.shape[1])], axis=1)


def scale_kernel(*refs):
    anchors = refs[:NX]
    totals = refs[NX : 2 * NX]
    out_ref = refs[2 * NX]
    n = out_ref.shape[0] // NX
    for b in range(NX):
        t = None
        for k in range(NX):
            at = ((b - k) % NX) * n
            piece = totals[k][:, at : at + n]
            t = piece if t is None else t + piece
        column = column_of((1.0 / TEMPER) * weights_of(anchors[b], n) / t)
        out_ref[b * n : (b + 1) * n, :] = (anchors[b][:n, :].astype(F32) * column).astype(BF)


def scale(anchors, totals, n):
    return vmem_call(
        scale_kernel,
        jax.ShapeDtypeStruct((NX * n, anchors[0].shape[1]), BF),
        "scale",
        in_specs=[IN_VMEM] * (2 * NX),
        out_specs=IN_VMEM,
    )(*anchors, *totals)


def mix_kernel(which, a_ref, *refs):
    parts, outs = refs[:NX], refs[NX:]
    for k, out in zip(which, outs):
        total = None
        for b, part in enumerate(parts):
            size = part.shape[2]
            term = jnp.dot(part[k], a_ref[b * size : (b + 1) * size, :], preferred_element_type=F32)
            total = term if total is None else total + term
        out[...] = total.astype(out.dtype)


def mix(which, scaled, parts, dtype):
    shape = jax.ShapeDtypeStruct((parts[0].shape[1], scaled.shape[1]), dtype)
    return vmem_call(
        functools.partial(mix_kernel, which),
        tuple(shape for _ in which),
        "mix",
        in_specs=[IN_VMEM] * (1 + NX),
        out_specs=tuple(IN_VMEM for _ in which),
    )(scaled, *parts)


def finish_kernel(
    core_ref,
    up_ref,
    down_ref,
    own_ref,
    message_ref,
    feats_ref,
    weight_ref,
    grad_ref,
    keep_ref,
    send_ref,
):
    n = up_ref.shape[0]
    feats = feats_ref[...]
    unit, inv = project(feats, weight_ref[...])
    mixed = own_ref[...] + up_ref[...].astype(F32) + down_ref[...].astype(F32)
    w = column_of((1.0 / TEMPER) * weights_of(message_ref, n))
    grad = mixed - w * message_ref[:n, :].astype(F32)
    along = jnp.sum(unit * grad, axis=1, keepdims=True)
    grad = ((grad - unit * along) * inv).astype(BF)
    grad_ref[...] = grad
    part = lax.dot_general(feats, grad, (((0,), (0,)), ((), ())), preferred_element_type=F32)
    half = keep_ref.shape[0]
    for core in range(NC):

        @pl.when(core_ref[0] == core)
        def _():
            keep_ref[...] = part[core * half : (core + 1) * half]
            send_ref[...] = part[(1 - core) * half : (2 - core) * half]


def finish(core, up, down, own, message, features, weight):
    n, width = up.shape
    half = jax.ShapeDtypeStruct((features.shape[1] // NC, width), F32)
    return vmem_call(
        finish_kernel,
        (jax.ShapeDtypeStruct((n, width), BF), half, half),
        "finish",
        in_specs=[pl.BlockSpec(memory_space=pltpu.SMEM)] + [IN_VMEM] * 6,
        out_specs=(IN_VMEM,) * 3,
    )(core.reshape(1), up, down, own, message, features, weight)


def sum_everywhere(keep, send, core, beside):
    rows, width = keep.shape
    v = keep + lax.ppermute(send, "core", flip(NC, 1))
    many = NY * NX
    v = lax.all_to_all(v, ("y", "x"), 0, 0, tiled=True)
    v = jnp.sum(v.reshape(many, rows // many, width), axis=0)
    got = [lax.ppermute(v, "z", flip(NZ, m)) for m in (1, 2, 3)]
    v = (v + got[0]) + (got[1] + got[2])
    v = v + lax.ppermute(v, "z", flip(NZ, 4))
    v, beside = lax.optimization_barrier((v, beside))
    v = lax.optimization_barrier(jnp.broadcast_to(v[None], (many,) + v.shape))
    v = lax.all_to_all(v.reshape(rows, width), ("y", "x"), 0, 0, tiled=True)
    other = lax.ppermute(v, "core", flip(NC, 1))
    low, high = jnp.where(core == 0, v, other), jnp.where(core == 0, other, v)
    return jnp.concatenate([low, high], axis=0), beside


def local(features, weight, support_queue, owner_shard, slot_row, loss_weight):
    n = features.shape[0]
    width = weight.shape[1]

    core = lax.axis_index("core")
    owner = owner_shard.reshape(1, n)
    view_bf, wanted = begin(features, weight, owner, slot_row.reshape(1, n))
    views = {0: view_bf}
    views[7] = lax.ppermute(view_bf, "z", shift(NZ, 1))
    views[1] = lax.ppermute(view_bf, "z", shift(NZ, -1))
    asked = lax.all_to_all(wanted, QUEUE, split_axis=0, concat_axis=0, tiled=True)
    asked, views[7], views[1] = lax.optimization_barrier((asked, views[7], views[1]))
    views[6] = lax.ppermute(views[7], "z", shift(NZ, 1))
    views[2] = lax.ppermute(views[1], "z", shift(NZ, -1))
    first = support_queue[asked[:, : CAP // 2]]
    first, views[6], views[2] = lax.optimization_barrier((first, views[6], views[2]))
    first = lax.all_to_all(first, QUEUE, split_axis=0, concat_axis=0, tiled=True)
    second = support_queue[asked[:, CAP // 2 :]]
    second = lax.all_to_all(second, QUEUE, split_axis=0, concat_axis=0, tiled=True)
    views[5] = lax.ppermute(views[6], "z", shift(NZ, 1))
    views[3] = lax.ppermute(views[2], "z", shift(NZ, -1))
    views[4] = lax.ppermute(views[5], "z", shift(NZ, 1))
    views = [views[d] for d in range(NZ)]

    extra = jnp.zeros((16, width), BF).at[: n // width].set(loss_weight.reshape(n // width, width))
    slots = NZ * NX * CAP // 2
    message = pick(first.reshape(slots, width), second.reshape(slots, width), owner, extra)

    blocks = [message] + [lax.ppermute(message, "x", shift(NX, k)) for k in (1, 2, 3)]
    parts, totals = {}, {}
    for b in (0, 1, 3, 2):
        parts[b], totals[b] = exps(blocks[b], views)
    parts = [parts[b] for b in range(NX)]
    total = jnp.concatenate([totals[b] for b in range(NX)], axis=1)
    everyone = [total] + [lax.ppermute(total, "x", shift(NX, k)) for k in (1, 2, 3)]
    scaled = scale(blocks, everyone, n)

    (far,) = mix((4,), scaled, parts, BF)
    up, down = far[: n // 2], far[n // 2 :]
    for d in (3, 2, 1):
        which = (d, NZ - d) if d > 1 else (d, NZ - d, 0)
        up_part, down_part, *rest = mix(which, scaled, parts, F32)
        up = lax.ppermute(up, "z", shift(NZ, 1)).astype(F32)
        down = lax.ppermute(down, "z", shift(NZ, -1)).astype(F32)
        if d == 3:
            up = jnp.concatenate([up + up_part[: n // 2], up_part[n // 2 :]], axis=0)
            down = jnp.concatenate([down_part[: n // 2], down + down_part[n // 2 :]], axis=0)
        else:
            up, down = up + up_part, down + down_part
        up, down = up.astype(BF), down.astype(BF)
    (own,) = rest
    up = lax.ppermute(up, "z", shift(NZ, 1))
    down = lax.ppermute(down, "z", shift(NZ, -1))

    grad_proj, keep, send = finish(core, up, down, own, message, features, weight)
    grad_feats = jnp.dot(grad_proj, weight.T, preferred_element_type=F32).astype(BF)
    grad_weight, grad_feats = sum_everywhere(keep, send, core, grad_feats)
    return (grad_feats, grad_weight)


def solution(mesh):
    mesh = Mesh(mesh.devices.reshape(NY, NC, NZ, NX), ("y", "core", "z", "x"))
    views = ("y", "core", "z", "x")
    in_specs = (
        P(views, None),
        P(),
        P(QUEUE, None),
        P(views, None),
        P(views),
        P(views),
    )
    out_specs = (P(views, None), P())
    return jax.shard_map(local, mesh=mesh, in_specs=in_specs, out_specs=out_specs, check_vma=False)
```

```python
import functools
import math

import jax
import jax.numpy as jnp
from jax import lax
from jax.experimental import pallas as pl
from jax.experimental.pallas import tpu as pltpu
from jax.sharding import Mesh
from jax.sharding import PartitionSpec as P

TEMPER = 0.1
EPSILON = 1e-06
NZ, NX, NY, NC = 8, 4, 4, 2
CAP = 64
BF = jnp.bfloat16
F32 = jnp.float32
VMEM_LIMIT = 16 * 1024 * 1024
ALL_VMEM = 62 * 1024 * 1024
IN_VMEM = pl.BlockSpec(memory_space=pltpu.VMEM)
EXPONENT = math.log2(math.e) / TEMPER
QUEUE = ("z", "x")


def shift(size, by):
    return [(i, (i + by) % size) for i in range(size)]


def flip(size, mask):
    return [(i, i ^ mask) for i in range(size)]


def vmem_call(kernel, out_shape, name, limit=VMEM_LIMIT, **kw):
    return pl.pallas_call(
        kernel,
        out_shape=out_shape,
        compiler_params=pltpu.CompilerParams(vmem_limit_bytes=limit),
        name=name,
        **kw,
    )


def ranks(owner, shards):
    n = owner.shape[1]
    onehot = jnp.where(owner == lax.broadcasted_iota(jnp.int32, (shards, n), 0), 1.0, 0.0)
    above = lax.broadcasted_iota(jnp.int32, (n, n), 0) < lax.broadcasted_iota(jnp.int32, (n, n), 1)
    above = jnp.where(above, 1.0, 0.0).astype(BF)
    before = jnp.dot(onehot.astype(BF), above, preferred_element_type=F32)
    return onehot, jnp.sum(before * onehot, axis=0, keepdims=True).astype(jnp.int32)


def project(features, weight):
    projected = jnp.dot(features, weight, preferred_element_type=F32)
    inv = lax.rsqrt(jnp.sum(projected * projected, axis=1, keepdims=True) + EPSILON)
    return projected * inv, inv


def begin_kernel(
    feats_hbm,
    weight_hbm,
    owner_hbm,
    slot_hbm,
    view_ref,
    wanted_ref,
    feats_ref,
    weight_ref,
    owner_ref,
    slot_ref,
    sems,
):
    copies = [
        pltpu.make_async_copy(owner_hbm, owner_ref, sems.at[0]),
        pltpu.make_async_copy(slot_hbm, slot_ref, sems.at[1]),
        pltpu.make_async_copy(weight_hbm, weight_ref, sems.at[2]),
        pltpu.make_async_copy(feats_hbm, feats_ref, sems.at[3]),
    ]
    for copy in copies:
        copy.start()
    copies[0].wait()
    copies[1].wait()
    n = owner_ref.shape[1]
    slot = slot_ref[...]
    onehot, rank = ranks(owner_ref[...], wanted_ref.shape[0])
    chosen = jnp.where(rank == lax.broadcasted_iota(jnp.int32, (128, n), 0), 1.0, 0.0).astype(BF)
    both = (((1,), (1,)), ((), ()))
    high = (onehot * (slot >> 7).astype(F32)).astype(BF)
    low = (onehot * (slot & 127).astype(F32)).astype(BF)
    upper = lax.dot_general(high, chosen, both, preferred_element_type=F32)
    lower = lax.dot_general(low, chosen, both, preferred_element_type=F32)
    full = upper.astype(jnp.int32) * 128 + lower.astype(jnp.int32)
    wanted_ref[...] = full[:, :CAP]
    copies[2].wait()
    copies[3].wait()
    view_ref[...] = project(feats_ref[...], weight_ref[...])[0].astype(BF)


def begin(features, weight, owner, slot):
    n, width = features.shape[0], weight.shape[1]
    in_hbm = pl.BlockSpec(memory_space=pltpu.HBM)
    return vmem_call(
        begin_kernel,
        (
            jax.ShapeDtypeStruct((n, width), BF),
            jax.ShapeDtypeStruct((NZ * NX, CAP), jnp.int32),
        ),
        "begin",
        ALL_VMEM,
        in_specs=[in_hbm] * 4,
        out_specs=(IN_VMEM, IN_VMEM),
        scratch_shapes=[
            pltpu.VMEM(features.shape, BF),
            pltpu.VMEM(weight.shape, BF),
            pltpu.VMEM(owner.shape, jnp.int32),
            pltpu.VMEM(slot.shape, jnp.int32),
            pltpu.SemaphoreType.DMA((4,)),
        ],
    )(features, weight, owner, slot)


def column_of(row):
    return jnp.broadcast_to(row, (8, row.shape[1])).T[:, :1]


def pick_kernel(rows_ref, owner_ref, extra_ref, out_ref):
    n = owner_ref.shape[1]
    owner = owner_ref[...]
    places = column_of(owner * CAP + ranks(owner, rows_ref.shape[0] // CAP)[1])
    column = lax.broadcasted_iota(jnp.int32, (n, n), 1)
    total = None
    for at in range(0, rows_ref.shape[0], n):
        onehot = jnp.where(places == column + at, 1.0, 0.0).astype(BF)
        term = jnp.dot(onehot, rows_ref[at : at + n, :], preferred_element_type=F32)
        total = term if total is None else total + term
    unit = total * lax.rsqrt(jnp.sum(total * total, axis=1, keepdims=True) + EPSILON)
    out_ref[:n, :] = unit.astype(BF)
    out_ref[n:, :] = extra_ref[...]


def pick(rows, owner, extra):
    n = owner.shape[1]
    return vmem_call(
        pick_kernel,
        jax.ShapeDtypeStruct((n + extra.shape[0], rows.shape[1]), BF),
        "pick",
        in_specs=[IN_VMEM] * 3,
        out_specs=IN_VMEM,
    )(rows, owner, extra)


def exps_kernel(a_ref, *refs):
    views, (e_ref, t_ref) = refs[:NZ], refs[NZ:]
    n = t_ref.shape[1]
    a = a_ref[:n, :]
    total = jnp.zeros((8, n), F32)
    for k in range(NZ):
        dots = lax.dot_general(
            views[k][...], a, (((1,), (1,)), ((), ())), preferred_element_type=F32
        )
        e = jnp.exp2(dots * EXPONENT)
        total = total + jnp.sum(e.reshape(n // 8, 8, n), axis=0)
        e_ref[k] = e.astype(BF)
    t_ref[...] = jnp.sum(total, axis=0, keepdims=True)


def exps(anchors, views):
    n = views[0].shape[0]
    return vmem_call(
        exps_kernel,
        (jax.ShapeDtypeStruct((NZ, n, n), BF), jax.ShapeDtypeStruct((1, n), F32)),
        "exps",
        in_specs=[IN_VMEM] * (1 + NZ),
        out_specs=(IN_VMEM, IN_VMEM),
    )(anchors, *views)


def weights_of(message_ref, n):
    w = message_ref[n : n + 16, :].astype(F32)
    return jnp.concatenate([w[k : k + 1, :] for k in range(n // w.shape[1])], axis=1)


def scale_kernel(*refs):
    anchors = refs[:NX]
    totals = refs[NX : 2 * NX]
    out_ref = refs[2 * NX]
    n = out_ref.shape[0] // NX
    for b in range(NX):
        t = None
        for k in range(NX):
            at = ((b - k) % NX) * n
            piece = totals[k][:, at : at + n]
            t = piece if t is None else t + piece
        column = column_of((1.0 / TEMPER) * weights_of(anchors[b], n) / t)
        out_ref[b * n : (b + 1) * n, :] = (anchors[b][:n, :].astype(F32) * column).astype(BF)


def scale(anchors, totals, n):
    return vmem_call(
        scale_kernel,
        jax.ShapeDtypeStruct((NX * n, anchors[0].shape[1]), BF),
        "scale",
        in_specs=[IN_VMEM] * (2 * NX),
        out_specs=IN_VMEM,
    )(*anchors, *totals)


def product(k, a_ref, parts):
    total = None
    for b, part in enumerate(parts):
        size = part.shape[2]
        term = jnp.dot(part[k], a_ref[b * size : (b + 1) * size, :], preferred_element_type=F32)
        total = term if total is None else total + term
    return total


def mix_kernel(which, a_ref, *refs):
    for k, out in zip(which, refs[NX:]):
        out[...] = product(k, a_ref, refs[:NX]).astype(out.dtype)


def far_kernel(a_ref, *refs):
    total = product(NZ // 2, a_ref, refs[:NX]).astype(BF)
    half = total.shape[0] // 2
    refs[NX][...] = total[:half]
    refs[NX + 1][...] = total[half:]


def mix_far(scaled, parts):
    shape = jax.ShapeDtypeStruct((parts[0].shape[1] // 2, scaled.shape[1]), BF)
    return vmem_call(
        far_kernel,
        (shape, shape),
        "mix_far",
        in_specs=[IN_VMEM] * (1 + NX),
        out_specs=(IN_VMEM, IN_VMEM),
    )(scaled, *parts)


def mix(which, scaled, parts, dtype):
    shape = jax.ShapeDtypeStruct((parts[0].shape[1], scaled.shape[1]), dtype)
    return vmem_call(
        functools.partial(mix_kernel, which),
        tuple(shape for _ in which),
        "mix",
        in_specs=[IN_VMEM] * (1 + NX),
        out_specs=tuple(IN_VMEM for _ in which),
    )(scaled, *parts)


def finish_kernel(
    core_ref,
    up_ref,
    down_ref,
    own_ref,
    message_ref,
    feats_ref,
    weight_ref,
    grad_ref,
    keep_ref,
    send_ref,
):
    n = up_ref.shape[0]
    feats = feats_ref[...]
    unit, inv = project(feats, weight_ref[...])
    mixed = own_ref[...] + up_ref[...].astype(F32) + down_ref[...].astype(F32)
    w = column_of((1.0 / TEMPER) * weights_of(message_ref, n))
    grad = mixed - w * message_ref[:n, :].astype(F32)
    along = jnp.sum(unit * grad, axis=1, keepdims=True)
    grad = ((grad - unit * along) * inv).astype(BF)
    grad_ref[...] = grad
    part = lax.dot_general(feats, grad, (((0,), (0,)), ((), ())), preferred_element_type=F32)
    half = keep_ref.shape[0]
    for core in range(NC):

        @pl.when(core_ref[0] == core)
        def _():
            keep_ref[...] = part[core * half : (core + 1) * half]
            send_ref[...] = part[(1 - core) * half : (2 - core) * half]


def finish(core, up, down, own, message, features, weight):
    n, width = up.shape
    half = jax.ShapeDtypeStruct((features.shape[1] // NC, width), F32)
    return vmem_call(
        finish_kernel,
        (jax.ShapeDtypeStruct((n, width), BF), half, half),
        "finish",
        in_specs=[pl.BlockSpec(memory_space=pltpu.SMEM)] + [IN_VMEM] * 6,
        out_specs=(IN_VMEM,) * 3,
    )(core.reshape(1), up, down, own, message, features, weight)


def sum_everywhere(keep, send, core, beside):
    rows, width = keep.shape
    v = keep + lax.ppermute(send, "core", flip(NC, 1))
    many = NY * NX
    v = lax.all_to_all(v.astype(BF), ("y", "x"), 0, 0, tiled=True).astype(F32)
    v = jnp.sum(v.reshape(many, rows // many, width), axis=0)
    got = [lax.ppermute(v, "z", flip(NZ, m)) for m in (1, 2, 3)]
    v = (v + got[0]) + (got[1] + got[2])
    v = v + lax.ppermute(v, "z", flip(NZ, 4))
    v, beside = lax.optimization_barrier((v.astype(BF), beside))
    v = lax.optimization_barrier(jnp.broadcast_to(v[None], (many,) + v.shape))
    v = lax.all_to_all(v.reshape(rows, width), ("y", "x"), 0, 0, tiled=True)
    other = lax.ppermute(v, "core", flip(NC, 1))
    low, high = jnp.where(core == 0, v, other), jnp.where(core == 0, other, v)
    return jnp.concatenate([low, high], axis=0).astype(F32), beside


def local(features, weight, support_queue, owner_shard, slot_row, loss_weight):
    n = features.shape[0]
    width = weight.shape[1]

    core = lax.axis_index("core")
    owner = owner_shard.reshape(1, n)
    view_bf, wanted = begin(features, weight, owner, slot_row.reshape(1, n))
    views = {0: view_bf}
    views[7] = lax.ppermute(view_bf, "z", shift(NZ, 1))
    views[1] = lax.ppermute(view_bf, "z", shift(NZ, -1))
    asked = lax.all_to_all(wanted, QUEUE, split_axis=0, concat_axis=0, tiled=True)
    asked, views[7], views[1] = lax.optimization_barrier((asked, views[7], views[1]))
    views[6] = lax.ppermute(views[7], "z", shift(NZ, 1))
    views[2] = lax.ppermute(views[1], "z", shift(NZ, -1))
    picked = support_queue[asked]
    picked, views[6], views[2] = lax.optimization_barrier((picked, views[6], views[2]))
    views[5] = lax.ppermute(views[6], "z", shift(NZ, 1))
    views[3] = lax.ppermute(views[2], "z", shift(NZ, -1))
    views[4] = lax.ppermute(views[5], "z", shift(NZ, 1))
    views = [views[d] for d in range(NZ)]

    answered = lax.all_to_all(picked, QUEUE, split_axis=0, concat_axis=0, tiled=True)
    extra = jnp.zeros((16, width), BF).at[: n // width].set(loss_weight.reshape(n // width, width))
    message = pick(answered.reshape(NZ * NX * CAP, width), owner, extra)

    blocks = [message] + [lax.ppermute(message, "x", shift(NX, k)) for k in (1, 2, 3)]
    parts, totals = {}, {}
    for b in (0, 1, 3, 2):
        parts[b], totals[b] = exps(blocks[b], views)
    parts = [parts[b] for b in range(NX)]
    total = jnp.concatenate([totals[b] for b in range(NX)], axis=1)
    everyone = [total] + [lax.ppermute(total, "x", shift(NX, k)) for k in (1, 2, 3)]
    scaled = scale(blocks, everyone, n)

    up, down = mix_far(scaled, parts)
    for d in (3, 2, 1):
        which = (d, NZ - d) if d > 1 else (d, NZ - d, 0)
        up_part, down_part, *rest = mix(which, scaled, parts, F32)
        up = lax.ppermute(up, "z", shift(NZ, 1)).astype(F32)
        down = lax.ppermute(down, "z", shift(NZ, -1)).astype(F32)
        if d == 3:
            up = jnp.concatenate([up + up_part[: n // 2], up_part[n // 2 :]], axis=0)
            down = jnp.concatenate([down_part[: n // 2], down + down_part[n // 2 :]], axis=0)
        else:
            up, down = up + up_part, down + down_part
        up, down = lax.optimization_barrier((up.astype(BF), down.astype(BF)))
    (own,) = rest
    up = lax.ppermute(up, "z", shift(NZ, 1))
    down = lax.ppermute(down, "z", shift(NZ, -1))

    grad_proj, keep, send = finish(core, up, down, own, message, features, weight)
    grad_feats = jnp.dot(grad_proj, weight.T, preferred_element_type=F32).astype(BF)
    grad_weight, grad_feats = sum_everywhere(keep, send, core, grad_feats)
    return (grad_feats, grad_weight)


def solution(mesh):
    mesh = Mesh(mesh.devices.reshape(NY, NC, NZ, NX), ("y", "core", "z", "x"))
    views = ("y", "core", "z", "x")
    in_specs = (
        P(views, None),
        P(),
        P(QUEUE, None),
        P(views, None),
        P(views),
        P(views),
    )
    out_specs = (P(views, None), P())
    return jax.shard_map(local, mesh=mesh, in_specs=in_specs, out_specs=out_specs, check_vma=False)
```

```python
import functools
import math

import jax
import jax.numpy as jnp
from jax import lax
from jax.experimental import pallas as pl
from jax.experimental.pallas import tpu as pltpu
from jax.sharding import Mesh
from jax.sharding import PartitionSpec as P

TEMPER = 0.1
EPSILON = 1e-06
NZ, NX, NY, NC = 8, 4, 4, 2
CAP = 64
BF = jnp.bfloat16
F32 = jnp.float32
VMEM_LIMIT = 16 * 1024 * 1024
ALL_VMEM = 62 * 1024 * 1024
IN_VMEM = pl.BlockSpec(memory_space=pltpu.VMEM)
EXPONENT = math.log2(math.e) / TEMPER
QUEUE = ("z", "x")


def shift(size, by):
    return [(i, (i + by) % size) for i in range(size)]


def flip(size, mask):
    return [(i, i ^ mask) for i in range(size)]


def vmem_call(kernel, out_shape, name, limit=VMEM_LIMIT, **kw):
    return pl.pallas_call(
        kernel,
        out_shape=out_shape,
        compiler_params=pltpu.CompilerParams(vmem_limit_bytes=limit),
        name=name,
        **kw,
    )


def ranks(owner, shards):
    n = owner.shape[1]
    onehot = jnp.where(owner == lax.broadcasted_iota(jnp.int32, (shards, n), 0), 1.0, 0.0)
    above = lax.broadcasted_iota(jnp.int32, (n, n), 0) < lax.broadcasted_iota(jnp.int32, (n, n), 1)
    above = jnp.where(above, 1.0, 0.0).astype(BF)
    before = jnp.dot(onehot.astype(BF), above, preferred_element_type=F32)
    return onehot, jnp.sum(before * onehot, axis=0, keepdims=True).astype(jnp.int32)


def project(features, weight):
    projected = jnp.dot(features, weight, preferred_element_type=F32)
    inv = lax.rsqrt(jnp.sum(projected * projected, axis=1, keepdims=True) + EPSILON)
    return projected * inv, inv


def begin_kernel(
    feats_hbm,
    weight_hbm,
    owner_hbm,
    slot_hbm,
    view_ref,
    wanted_ref,
    feats_ref,
    weight_ref,
    owner_ref,
    slot_ref,
    sems,
):
    copies = [
        pltpu.make_async_copy(owner_hbm, owner_ref, sems.at[0]),
        pltpu.make_async_copy(slot_hbm, slot_ref, sems.at[1]),
        pltpu.make_async_copy(weight_hbm, weight_ref, sems.at[2]),
        pltpu.make_async_copy(feats_hbm, feats_ref, sems.at[3]),
    ]
    for copy in copies:
        copy.start()
    copies[0].wait()
    copies[1].wait()
    n = owner_ref.shape[1]
    slot = slot_ref[...]
    onehot, rank = ranks(owner_ref[...], wanted_ref.shape[0])
    chosen = jnp.where(rank == lax.broadcasted_iota(jnp.int32, (128, n), 0), 1.0, 0.0).astype(BF)
    both = (((1,), (1,)), ((), ()))
    high = (onehot * (slot >> 7).astype(F32)).astype(BF)
    low = (onehot * (slot & 127).astype(F32)).astype(BF)
    upper = lax.dot_general(high, chosen, both, preferred_element_type=F32)
    lower = lax.dot_general(low, chosen, both, preferred_element_type=F32)
    full = upper.astype(jnp.int32) * 128 + lower.astype(jnp.int32)
    wanted_ref[...] = full[:, :CAP]
    copies[2].wait()
    copies[3].wait()
    view_ref[...] = project(feats_ref[...], weight_ref[...])[0].astype(BF)


def begin(features, weight, owner, slot):
    n, width = features.shape[0], weight.shape[1]
    in_hbm = pl.BlockSpec(memory_space=pltpu.HBM)
    return vmem_call(
        begin_kernel,
        (
            jax.ShapeDtypeStruct((n, width), BF),
            jax.ShapeDtypeStruct((NZ * NX, CAP), jnp.int32),
        ),
        "begin",
        ALL_VMEM,
        in_specs=[in_hbm] * 4,
        out_specs=(IN_VMEM, IN_VMEM),
        scratch_shapes=[
            pltpu.VMEM(features.shape, BF),
            pltpu.VMEM(weight.shape, BF),
            pltpu.VMEM(owner.shape, jnp.int32),
            pltpu.VMEM(slot.shape, jnp.int32),
            pltpu.SemaphoreType.DMA((4,)),
        ],
    )(features, weight, owner, slot)


def column_of(row):
    return jnp.broadcast_to(row, (8, row.shape[1])).T[:, :1]


def pick_kernel(rows_ref, owner_ref, extra_ref, out_ref):
    n = owner_ref.shape[1]
    owner = owner_ref[...]
    places = column_of(owner * CAP + ranks(owner, rows_ref.shape[0] // CAP)[1])
    column = lax.broadcasted_iota(jnp.int32, (n, n), 1)
    total = None
    for at in range(0, rows_ref.shape[0], n):
        onehot = jnp.where(places == column + at, 1.0, 0.0).astype(BF)
        term = jnp.dot(onehot, rows_ref[at : at + n, :], preferred_element_type=F32)
        total = term if total is None else total + term
    unit = total * lax.rsqrt(jnp.sum(total * total, axis=1, keepdims=True) + EPSILON)
    out_ref[:n, :] = unit.astype(BF)
    out_ref[n:, :] = extra_ref[...]


def pick(rows, owner, extra):
    n = owner.shape[1]
    return vmem_call(
        pick_kernel,
        jax.ShapeDtypeStruct((n + extra.shape[0], rows.shape[1]), BF),
        "pick",
        in_specs=[IN_VMEM] * 3,
        out_specs=IN_VMEM,
    )(rows, owner, extra)


def exps_kernel(a_ref, *refs):
    views, (e_ref, t_ref) = refs[:NZ], refs[NZ:]
    n = t_ref.shape[1]
    a = a_ref[:n, :]
    total = jnp.zeros((8, n), F32)
    for k in range(NZ):
        dots = lax.dot_general(
            views[k][...], a, (((1,), (1,)), ((), ())), preferred_element_type=F32
        )
        e = jnp.exp2(dots * EXPONENT)
        total = total + jnp.sum(e.reshape(n // 8, 8, n), axis=0)
        e_ref[k] = e.astype(BF)
    t_ref[...] = jnp.sum(total, axis=0, keepdims=True)


def exps(anchors, views):
    n = views[0].shape[0]
    return vmem_call(
        exps_kernel,
        (jax.ShapeDtypeStruct((NZ, n, n), BF), jax.ShapeDtypeStruct((1, n), F32)),
        "exps",
        in_specs=[IN_VMEM] * (1 + NZ),
        out_specs=(IN_VMEM, IN_VMEM),
    )(anchors, *views)


def weights_of(message_ref, n):
    w = message_ref[n : n + 16, :].astype(F32)
    return jnp.concatenate([w[k : k + 1, :] for k in range(n // w.shape[1])], axis=1)


def scale_kernel(*refs):
    anchors = refs[:NX]
    totals = refs[NX : 2 * NX]
    out_ref = refs[2 * NX]
    n = out_ref.shape[0] // NX
    for b in range(NX):
        t = None
        for k in range(NX):
            at = ((b - k) % NX) * n
            piece = totals[k][:, at : at + n]
            t = piece if t is None else t + piece
        column = column_of((1.0 / TEMPER) * weights_of(anchors[b], n) / t)
        out_ref[b * n : (b + 1) * n, :] = (anchors[b][:n, :].astype(F32) * column).astype(BF)


def scale(anchors, totals, n):
    return vmem_call(
        scale_kernel,
        jax.ShapeDtypeStruct((NX * n, anchors[0].shape[1]), BF),
        "scale",
        in_specs=[IN_VMEM] * (2 * NX),
        out_specs=IN_VMEM,
    )(*anchors, *totals)


def product(k, a_ref, parts):
    total = None
    for b, part in enumerate(parts):
        size = part.shape[2]
        term = jnp.dot(part[k], a_ref[b * size : (b + 1) * size, :], preferred_element_type=F32)
        total = term if total is None else total + term
    return total


def mix_kernel(which, a_ref, *refs):
    outs = iter(refs[NX:])
    for k in which:
        total = product(k, a_ref, refs[:NX])
        half = total.shape[0] // 2
        for h in range(2):
            out = next(outs)
            out[...] = total[h * half : (h + 1) * half].astype(out.dtype)


def mix(which, scaled, parts, dtype):
    shape = jax.ShapeDtypeStruct((parts[0].shape[1] // 2, scaled.shape[1]), dtype)
    return vmem_call(
        functools.partial(mix_kernel, which),
        (shape,) * (2 * len(which)),
        "mix",
        in_specs=[IN_VMEM] * (1 + NX),
        out_specs=(IN_VMEM,) * (2 * len(which)),
    )(scaled, *parts)


def finish_kernel(core_ref, *refs):
    halves, (message_ref, feats_ref, weight_ref, grad_ref, keep_ref, send_ref) = refs[:6], refs[6:]
    n = feats_ref.shape[0]
    feats = feats_ref[...]
    unit, inv = project(feats, weight_ref[...])
    mixed = jnp.concatenate(
        [sum(halves[2 * k + h][...].astype(F32) for k in range(3)) for h in range(2)], axis=0
    )
    w = column_of((1.0 / TEMPER) * weights_of(message_ref, n))
    grad = mixed - w * message_ref[:n, :].astype(F32)
    along = jnp.sum(unit * grad, axis=1, keepdims=True)
    grad = ((grad - unit * along) * inv).astype(BF)
    grad_ref[...] = grad
    part = lax.dot_general(feats, grad, (((0,), (0,)), ((), ())), preferred_element_type=F32)
    half = keep_ref.shape[0]
    for core in range(NC):

        @pl.when(core_ref[0] == core)
        def _():
            keep_ref[...] = part[core * half : (core + 1) * half]
            send_ref[...] = part[(1 - core) * half : (2 - core) * half]


def finish(core, ups, downs, own, message, features, weight):
    n, width = features.shape[0], weight.shape[1]
    half = jax.ShapeDtypeStruct((features.shape[1] // NC, width), F32)
    return vmem_call(
        finish_kernel,
        (jax.ShapeDtypeStruct((n, width), BF), half, half),
        "finish",
        in_specs=[pl.BlockSpec(memory_space=pltpu.SMEM)] + [IN_VMEM] * 9,
        out_specs=(IN_VMEM,) * 3,
    )(core.reshape(1), *own, *ups, *downs, message, features, weight)


def sum_everywhere(keep, send, core, beside):
    rows, width = keep.shape
    v = keep + lax.ppermute(send, "core", flip(NC, 1))
    many = NY * NX
    v = lax.all_to_all(v.astype(BF), ("y", "x"), 0, 0, tiled=True).astype(F32)
    v = jnp.sum(v.reshape(many, rows // many, width), axis=0)
    got = [lax.ppermute(v, "z", flip(NZ, m)) for m in (1, 2, 3)]
    v = (v + got[0]) + (got[1] + got[2])
    v = v + lax.ppermute(v, "z", flip(NZ, 4))
    v, beside = lax.optimization_barrier((v.astype(BF), beside))
    v = lax.optimization_barrier(jnp.broadcast_to(v[None], (many,) + v.shape))
    v = lax.all_to_all(v.reshape(rows, width), ("y", "x"), 0, 0, tiled=True)
    other = lax.ppermute(v, "core", flip(NC, 1))
    low, high = jnp.where(core == 0, v, other), jnp.where(core == 0, other, v)
    return jnp.concatenate([low, high], axis=0).astype(F32), beside


def local(features, weight, support_queue, owner_shard, slot_row, loss_weight):
    n = features.shape[0]
    width = weight.shape[1]

    core = lax.axis_index("core")
    owner = owner_shard.reshape(1, n)
    view_bf, wanted = begin(features, weight, owner, slot_row.reshape(1, n))
    views = {0: view_bf}
    views[7] = lax.ppermute(view_bf, "z", shift(NZ, 1))
    views[1] = lax.ppermute(view_bf, "z", shift(NZ, -1))
    asked = lax.all_to_all(wanted, QUEUE, split_axis=0, concat_axis=0, tiled=True)
    asked, views[7], views[1] = lax.optimization_barrier((asked, views[7], views[1]))
    views[6] = lax.ppermute(views[7], "z", shift(NZ, 1))
    views[2] = lax.ppermute(views[1], "z", shift(NZ, -1))
    picked = support_queue[asked]
    picked, views[6], views[2] = lax.optimization_barrier((picked, views[6], views[2]))
    views[5] = lax.ppermute(views[6], "z", shift(NZ, 1))
    views[3] = lax.ppermute(views[2], "z", shift(NZ, -1))
    views[4] = lax.ppermute(views[5], "z", shift(NZ, 1))
    views = [views[d] for d in range(NZ)]

    answered = lax.all_to_all(picked, QUEUE, split_axis=0, concat_axis=0, tiled=True)
    extra = jnp.zeros((16, width), BF).at[: n // width].set(loss_weight.reshape(n // width, width))
    message = pick(answered.reshape(NZ * NX * CAP, width), owner, extra)

    blocks = [message] + [lax.ppermute(message, "x", shift(NX, k)) for k in (1, 2, 3)]
    parts, totals = {}, {}
    for b in (0, 1, 3, 2):
        parts[b], totals[b] = exps(blocks[b], views)
    parts = [parts[b] for b in range(NX)]
    total = jnp.concatenate([totals[b] for b in range(NX)], axis=1)
    everyone = [total] + [lax.ppermute(total, "x", shift(NX, k)) for k in (1, 2, 3)]
    scaled = scale(blocks, everyone, n)

    def hop(v, by, part):
        return (lax.ppermute(v, "z", shift(NZ, by)).astype(F32) + part).astype(BF)

    far = mix((NZ // 2,), scaled, parts, BF)
    up0, up1, down0, down1 = mix((3, NZ - 3), scaled, parts, F32)
    ups, downs = [hop(far[0], 1, up0), up1.astype(BF)], [down0.astype(BF), hop(far[1], -1, down1)]
    for d in (2, 1):
        which = (d, NZ - d) if d > 1 else (d, NZ - d, 0)
        up0, up1, down0, down1, *own = mix(which, scaled, parts, F32)
        ups = [hop(ups[0], 1, up0), hop(ups[1], 1, up1)]
        downs = [hop(downs[0], -1, down0), hop(downs[1], -1, down1)]
    ups = [lax.ppermute(v, "z", shift(NZ, 1)) for v in ups]
    downs = [lax.ppermute(v, "z", shift(NZ, -1)) for v in downs]

    grad_proj, keep, send = finish(core, ups, downs, own, message, features, weight)
    grad_feats = jnp.dot(grad_proj, weight.T, preferred_element_type=F32).astype(BF)
    grad_weight, grad_feats = sum_everywhere(keep, send, core, grad_feats)
    return (grad_feats, grad_weight)


def solution(mesh):
    mesh = Mesh(mesh.devices.reshape(NY, NC, NZ, NX), ("y", "core", "z", "x"))
    views = ("y", "core", "z", "x")
    in_specs = (
        P(views, None),
        P(),
        P(QUEUE, None),
        P(views, None),
        P(views),
        P(views),
    )
    out_specs = (P(views, None), P())
    return jax.shard_map(local, mesh=mesh, in_specs=in_specs, out_specs=out_specs, check_vma=False)
```

```python
import functools
import math

import jax
import jax.numpy as jnp
from jax import lax
from jax.experimental import pallas as pl
from jax.experimental.pallas import tpu as pltpu
from jax.sharding import Mesh
from jax.sharding import PartitionSpec as P

TEMPER = 0.1
EPSILON = 1e-06
NZ, NX, NY, NC = 8, 4, 4, 2
CAP = 64
BF = jnp.bfloat16
F32 = jnp.float32
VMEM_LIMIT = 16 * 1024 * 1024
ALL_VMEM = 62 * 1024 * 1024
IN_VMEM = pl.BlockSpec(memory_space=pltpu.VMEM)
EXPONENT = math.log2(math.e) / TEMPER
QUEUE = ("z", "x")


def shift(size, by):
    return [(i, (i + by) % size) for i in range(size)]


def flip(size, mask):
    return [(i, i ^ mask) for i in range(size)]


def vmem_call(kernel, out_shape, name, limit=VMEM_LIMIT, **kw):
    return pl.pallas_call(
        kernel,
        out_shape=out_shape,
        compiler_params=pltpu.CompilerParams(vmem_limit_bytes=limit),
        name=name,
        **kw,
    )


def ranks(owner, shards):
    n = owner.shape[1]
    onehot = jnp.where(owner == lax.broadcasted_iota(jnp.int32, (shards, n), 0), 1.0, 0.0)
    above = lax.broadcasted_iota(jnp.int32, (n, n), 0) < lax.broadcasted_iota(jnp.int32, (n, n), 1)
    above = jnp.where(above, 1.0, 0.0).astype(BF)
    before = jnp.dot(onehot.astype(BF), above, preferred_element_type=F32)
    return onehot, jnp.sum(before * onehot, axis=0, keepdims=True).astype(jnp.int32)


def project(features, weight):
    projected = jnp.dot(features, weight, preferred_element_type=F32)
    inv = lax.rsqrt(jnp.sum(projected * projected, axis=1, keepdims=True) + EPSILON)
    return projected * inv, inv


def begin_kernel(
    feats_hbm,
    weight_hbm,
    owner_hbm,
    slot_hbm,
    view_ref,
    wanted_ref,
    feats_ref,
    weight_ref,
    owner_ref,
    slot_ref,
    sems,
):
    copies = [
        pltpu.make_async_copy(owner_hbm, owner_ref, sems.at[0]),
        pltpu.make_async_copy(slot_hbm, slot_ref, sems.at[1]),
        pltpu.make_async_copy(weight_hbm, weight_ref, sems.at[2]),
        pltpu.make_async_copy(feats_hbm, feats_ref, sems.at[3]),
    ]
    for copy in copies:
        copy.start()
    copies[0].wait()
    copies[1].wait()
    n = owner_ref.shape[1]
    slot = slot_ref[...]
    onehot, rank = ranks(owner_ref[...], wanted_ref.shape[0])
    chosen = jnp.where(rank == lax.broadcasted_iota(jnp.int32, (128, n), 0), 1.0, 0.0).astype(BF)
    both = (((1,), (1,)), ((), ()))
    high = (onehot * (slot >> 7).astype(F32)).astype(BF)
    low = (onehot * (slot & 127).astype(F32)).astype(BF)
    upper = lax.dot_general(high, chosen, both, preferred_element_type=F32)
    lower = lax.dot_general(low, chosen, both, preferred_element_type=F32)
    full = upper.astype(jnp.int32) * 128 + lower.astype(jnp.int32)
    wanted_ref[...] = full[:, :CAP]
    copies[2].wait()
    copies[3].wait()
    view_ref[...] = project(feats_ref[...], weight_ref[...])[0].astype(BF)


def begin(features, weight, owner, slot):
    n, width = features.shape[0], weight.shape[1]
    in_hbm = pl.BlockSpec(memory_space=pltpu.HBM)
    return vmem_call(
        begin_kernel,
        (
            jax.ShapeDtypeStruct((n, width), BF),
            jax.ShapeDtypeStruct((NZ * NX, CAP), jnp.int32),
        ),
        "begin",
        ALL_VMEM,
        in_specs=[in_hbm] * 4,
        out_specs=(IN_VMEM, IN_VMEM),
        scratch_shapes=[
            pltpu.VMEM(features.shape, BF),
            pltpu.VMEM(weight.shape, BF),
            pltpu.VMEM(owner.shape, jnp.int32),
            pltpu.VMEM(slot.shape, jnp.int32),
            pltpu.SemaphoreType.DMA((4,)),
        ],
    )(features, weight, owner, slot)


def column_of(row):
    return jnp.broadcast_to(row, (8, row.shape[1])).T[:, :1]


def pick_kernel(rows_ref, owner_ref, extra_ref, out_ref):
    n = owner_ref.shape[1]
    owner = owner_ref[...]
    places = column_of(owner * CAP + ranks(owner, rows_ref.shape[0] // CAP)[1])
    column = lax.broadcasted_iota(jnp.int32, (n, n), 1)
    total = None
    for at in range(0, rows_ref.shape[0], n):
        onehot = jnp.where(places == column + at, 1.0, 0.0).astype(BF)
        term = jnp.dot(onehot, rows_ref[at : at + n, :], preferred_element_type=F32)
        total = term if total is None else total + term
    unit = total * lax.rsqrt(jnp.sum(total * total, axis=1, keepdims=True) + EPSILON)
    out_ref[:n, :] = unit.astype(BF)
    out_ref[n:, :] = extra_ref[...]


def pick(rows, owner, extra):
    n = owner.shape[1]
    return vmem_call(
        pick_kernel,
        jax.ShapeDtypeStruct((n + extra.shape[0], rows.shape[1]), BF),
        "pick",
        in_specs=[IN_VMEM] * 3,
        out_specs=IN_VMEM,
    )(rows, owner, extra)


def exps_kernel(a_ref, *refs):
    views, (e_ref, t_ref) = refs[:NZ], refs[NZ:]
    n = t_ref.shape[1]
    a = a_ref[:n, :]
    total = jnp.zeros((8, n), F32)
    for k in range(NZ):
        dots = lax.dot_general(
            views[k][...], a, (((1,), (1,)), ((), ())), preferred_element_type=F32
        )
        e = jnp.exp2(dots * EXPONENT)
        total = total + jnp.sum(e.reshape(n // 8, 8, n), axis=0)
        e_ref[k] = e.astype(BF)
    t_ref[...] = jnp.sum(total, axis=0, keepdims=True)


def exps(anchors, views):
    n = views[0].shape[0]
    return vmem_call(
        exps_kernel,
        (jax.ShapeDtypeStruct((NZ, n, n), BF), jax.ShapeDtypeStruct((1, n), F32)),
        "exps",
        in_specs=[IN_VMEM] * (1 + NZ),
        out_specs=(IN_VMEM, IN_VMEM),
    )(anchors, *views)


def weights_of(message_ref, n):
    w = message_ref[n : n + 16, :].astype(F32)
    return jnp.concatenate([w[k : k + 1, :] for k in range(n // w.shape[1])], axis=1)


def scale_kernel(*refs):
    anchors = refs[:NX]
    totals = refs[NX : 2 * NX]
    out_ref = refs[2 * NX]
    n = out_ref.shape[0] // NX
    for b in range(NX):
        t = None
        for k in range(NX):
            at = ((b - k) % NX) * n
            piece = totals[k][:, at : at + n]
            t = piece if t is None else t + piece
        column = column_of((1.0 / TEMPER) * weights_of(anchors[b], n) / t)
        out_ref[b * n : (b + 1) * n, :] = (anchors[b][:n, :].astype(F32) * column).astype(BF)


def scale(anchors, totals, n):
    return vmem_call(
        scale_kernel,
        jax.ShapeDtypeStruct((NX * n, anchors[0].shape[1]), BF),
        "scale",
        in_specs=[IN_VMEM] * (2 * NX),
        out_specs=IN_VMEM,
    )(*anchors, *totals)


def mix_kernel(a_ref, *refs):
    parts = refs[:NX]
    out_ref, up_ref, down_ref = refs[NX:]
    half = up_ref.shape[0]

    def one(k, carry):
        total = None
        for b, part in enumerate(parts):
            size = part.shape[2]
            term = jnp.dot(part[k], a_ref[b * size : (b + 1) * size, :], preferred_element_type=F32)
            total = term if total is None else total + term
        out_ref[k] = total
        return carry

    lax.fori_loop(0, NZ, one, 0)
    up_ref[...] = out_ref[NZ // 2, :half].astype(BF)
    down_ref[...] = out_ref[NZ // 2, half:].astype(BF)


def mix(scaled, parts):
    n, width = parts[0].shape[1], scaled.shape[1]
    half = jax.ShapeDtypeStruct((n // 2, width), BF)
    return vmem_call(
        mix_kernel,
        (jax.ShapeDtypeStruct((NZ, n, width), F32), half, half),
        "mix",
        in_specs=[IN_VMEM] * (1 + NX),
        out_specs=(IN_VMEM,) * 3,
    )(scaled, *parts)


def finish_kernel(
    core_ref,
    up_ref,
    down_ref,
    own_ref,
    message_ref,
    feats_ref,
    weight_ref,
    grad_ref,
    keep_ref,
    send_ref,
):
    n = up_ref.shape[0]
    feats = feats_ref[...]
    unit, inv = project(feats, weight_ref[...])
    mixed = own_ref[0] + up_ref[...].astype(F32) + down_ref[...].astype(F32)
    w = column_of((1.0 / TEMPER) * weights_of(message_ref, n))
    grad = mixed - w * message_ref[:n, :].astype(F32)
    along = jnp.sum(unit * grad, axis=1, keepdims=True)
    grad = ((grad - unit * along) * inv).astype(BF)
    grad_ref[...] = grad
    part = lax.dot_general(feats, grad, (((0,), (0,)), ((), ())), preferred_element_type=F32)
    half = keep_ref.shape[0]
    for core in range(NC):

        @pl.when(core_ref[0] == core)
        def _():
            keep_ref[...] = part[core * half : (core + 1) * half]
            send_ref[...] = part[(1 - core) * half : (2 - core) * half]


def finish(core, up, down, own, message, features, weight):
    n, width = up.shape
    half = jax.ShapeDtypeStruct((features.shape[1] // NC, width), F32)
    return vmem_call(
        finish_kernel,
        (jax.ShapeDtypeStruct((n, width), BF), half, half),
        "finish",
        in_specs=[pl.BlockSpec(memory_space=pltpu.SMEM)] + [IN_VMEM] * 6,
        out_specs=(IN_VMEM,) * 3,
    )(core.reshape(1), up, down, own, message, features, weight)


def sum_everywhere(keep, send, core, beside):
    rows, width = keep.shape
    v = keep + lax.ppermute(send, "core", flip(NC, 1))
    many = NY * NX
    v = lax.all_to_all(v.astype(BF), ("y", "x"), 0, 0, tiled=True).astype(F32)
    v = jnp.sum(v.reshape(many, rows // many, width), axis=0)
    got = [lax.ppermute(v, "z", flip(NZ, m)) for m in (1, 2, 3)]
    v = (v + got[0]) + (got[1] + got[2])
    v = v + lax.ppermute(v, "z", flip(NZ, 4))
    v, beside = lax.optimization_barrier((v.astype(BF), beside))
    v = lax.optimization_barrier(jnp.broadcast_to(v[None], (many,) + v.shape))
    v = lax.all_to_all(v.reshape(rows, width), ("y", "x"), 0, 0, tiled=True)
    other = lax.ppermute(v, "core", flip(NC, 1))
    low, high = jnp.where(core == 0, v, other), jnp.where(core == 0, other, v)
    return jnp.concatenate([low, high], axis=0).astype(F32), beside


def local(features, weight, support_queue, owner_shard, slot_row, loss_weight):
    n = features.shape[0]
    width = weight.shape[1]

    core = lax.axis_index("core")
    owner = owner_shard.reshape(1, n)
    view_bf, wanted = begin(features, weight, owner, slot_row.reshape(1, n))
    views = {0: view_bf}
    views[7] = lax.ppermute(view_bf, "z", shift(NZ, 1))
    views[1] = lax.ppermute(view_bf, "z", shift(NZ, -1))
    asked = lax.all_to_all(wanted, QUEUE, split_axis=0, concat_axis=0, tiled=True)
    asked, views[7], views[1] = lax.optimization_barrier((asked, views[7], views[1]))
    views[6] = lax.ppermute(views[7], "z", shift(NZ, 1))
    views[2] = lax.ppermute(views[1], "z", shift(NZ, -1))
    picked = support_queue[asked]
    picked, views[6], views[2] = lax.optimization_barrier((picked, views[6], views[2]))
    views[5] = lax.ppermute(views[6], "z", shift(NZ, 1))
    views[3] = lax.ppermute(views[2], "z", shift(NZ, -1))
    views[4] = lax.ppermute(views[5], "z", shift(NZ, 1))
    views = [views[d] for d in range(NZ)]

    answered = lax.all_to_all(picked, QUEUE, split_axis=0, concat_axis=0, tiled=True)
    extra = jnp.zeros((16, width), BF).at[: n // width].set(loss_weight.reshape(n // width, width))
    message = pick(answered.reshape(NZ * NX * CAP, width), owner, extra)

    blocks = [message] + [lax.ppermute(message, "x", shift(NX, k)) for k in (1, 2, 3)]
    parts, totals = {}, {}
    for b in (0, 1, 3, 2):
        parts[b], totals[b] = exps(blocks[b], views)
    parts = [parts[b] for b in range(NX)]
    total = jnp.concatenate([totals[b] for b in range(NX)], axis=1)
    everyone = [total] + [lax.ppermute(total, "x", shift(NX, k)) for k in (1, 2, 3)]
    scaled = scale(blocks, everyone, n)

    mixed, up, down = mix(scaled, parts)
    for d in (3, 2, 1):
        up_part, down_part = mixed[d], mixed[NZ - d]
        up = lax.ppermute(up, "z", shift(NZ, 1)).astype(F32)
        down = lax.ppermute(down, "z", shift(NZ, -1)).astype(F32)
        if d == 3:
            up = jnp.concatenate([up + up_part[: n // 2], up_part[n // 2 :]], axis=0)
            down = jnp.concatenate([down_part[: n // 2], down + down_part[n // 2 :]], axis=0)
        else:
            up, down = up + up_part, down + down_part
        up, down = lax.optimization_barrier((up.astype(BF), down.astype(BF)))
    up = lax.ppermute(up, "z", shift(NZ, 1))
    down = lax.ppermute(down, "z", shift(NZ, -1))

    grad_proj, keep, send = finish(core, up, down, mixed, message, features, weight)
    grad_feats = jnp.dot(grad_proj, weight.T, preferred_element_type=F32).astype(BF)
    grad_weight, grad_feats = sum_everywhere(keep, send, core, grad_feats)
    return (grad_feats, grad_weight)


def solution(mesh):
    mesh = Mesh(mesh.devices.reshape(NY, NC, NZ, NX), ("y", "core", "z", "x"))
    views = ("y", "core", "z", "x")
    in_specs = (
        P(views, None),
        P(),
        P(QUEUE, None),
        P(views, None),
        P(views),
        P(views),
    )
    out_specs = (P(views, None), P())
    return jax.shard_map(local, mesh=mesh, in_specs=in_specs, out_specs=out_specs, check_vma=False)
```

```python
import functools
import math

import jax
import jax.numpy as jnp
from jax import lax
from jax.experimental import pallas as pl
from jax.experimental.pallas import tpu as pltpu
from jax.sharding import Mesh
from jax.sharding import PartitionSpec as P

TEMPER = 0.1
EPSILON = 1e-06
NZ, NX, NY, NC = 8, 4, 4, 2
CAP = 64
BF = jnp.bfloat16
F32 = jnp.float32
VMEM_LIMIT = 16 * 1024 * 1024
ALL_VMEM = 62 * 1024 * 1024
IN_VMEM = pl.BlockSpec(memory_space=pltpu.VMEM)
EXPONENT = math.log2(math.e) / TEMPER
QUEUE = ("z", "x")


def shift(size, by):
    return [(i, (i + by) % size) for i in range(size)]


def flip(size, mask):
    return [(i, i ^ mask) for i in range(size)]


def vmem_call(kernel, out_shape, name, limit=VMEM_LIMIT, **kw):
    return pl.pallas_call(
        kernel,
        out_shape=out_shape,
        compiler_params=pltpu.CompilerParams(vmem_limit_bytes=limit),
        name=name,
        **kw,
    )


def ranks(owner, shards):
    n = owner.shape[1]
    onehot = jnp.where(owner == lax.broadcasted_iota(jnp.int32, (shards, n), 0), 1.0, 0.0)
    above = lax.broadcasted_iota(jnp.int32, (n, n), 0) < lax.broadcasted_iota(jnp.int32, (n, n), 1)
    above = jnp.where(above, 1.0, 0.0).astype(BF)
    before = jnp.dot(onehot.astype(BF), above, preferred_element_type=F32)
    return onehot, jnp.sum(before * onehot, axis=0, keepdims=True).astype(jnp.int32)


def project(features, weight):
    projected = jnp.dot(features, weight, preferred_element_type=F32)
    inv = lax.rsqrt(jnp.sum(projected * projected, axis=1, keepdims=True) + EPSILON)
    return projected * inv, inv


def begin_kernel(
    feats_hbm,
    weight_hbm,
    owner_hbm,
    slot_hbm,
    view_ref,
    wanted_ref,
    feats_ref,
    weight_ref,
    owner_ref,
    slot_ref,
    sems,
):
    copies = [
        pltpu.make_async_copy(owner_hbm, owner_ref, sems.at[0]),
        pltpu.make_async_copy(slot_hbm, slot_ref, sems.at[1]),
        pltpu.make_async_copy(weight_hbm, weight_ref, sems.at[2]),
        pltpu.make_async_copy(feats_hbm, feats_ref, sems.at[3]),
    ]
    for copy in copies:
        copy.start()
    copies[0].wait()
    copies[1].wait()
    n = owner_ref.shape[1]
    slot = slot_ref[...]
    onehot, rank = ranks(owner_ref[...], wanted_ref.shape[0])
    chosen = jnp.where(rank == lax.broadcasted_iota(jnp.int32, (128, n), 0), 1.0, 0.0).astype(BF)
    both = (((1,), (1,)), ((), ()))
    high = (onehot * (slot >> 7).astype(F32)).astype(BF)
    low = (onehot * (slot & 127).astype(F32)).astype(BF)
    upper = lax.dot_general(high, chosen, both, preferred_element_type=F32)
    lower = lax.dot_general(low, chosen, both, preferred_element_type=F32)
    full = upper.astype(jnp.int32) * 128 + lower.astype(jnp.int32)
    wanted_ref[...] = full[:, :CAP]
    copies[2].wait()
    copies[3].wait()
    view_ref[...] = project(feats_ref[...], weight_ref[...])[0].astype(BF)


def begin(features, weight, owner, slot):
    n, width = features.shape[0], weight.shape[1]
    in_hbm = pl.BlockSpec(memory_space=pltpu.HBM)
    return vmem_call(
        begin_kernel,
        (
            jax.ShapeDtypeStruct((n, width), BF),
            jax.ShapeDtypeStruct((NZ * NX, CAP), jnp.int32),
        ),
        "begin",
        ALL_VMEM,
        in_specs=[in_hbm] * 4,
        out_specs=(IN_VMEM, IN_VMEM),
        scratch_shapes=[
            pltpu.VMEM(features.shape, BF),
            pltpu.VMEM(weight.shape, BF),
            pltpu.VMEM(owner.shape, jnp.int32),
            pltpu.VMEM(slot.shape, jnp.int32),
            pltpu.SemaphoreType.DMA((4,)),
        ],
    )(features, weight, owner, slot)


def column_of(row):
    return jnp.broadcast_to(row, (8, row.shape[1])).T[:, :1]


def pick_kernel(rows_ref, owner_ref, extra_ref, out_ref):
    n = owner_ref.shape[1]
    owner = owner_ref[...]
    places = column_of(owner * CAP + ranks(owner, rows_ref.shape[0] // CAP)[1])
    column = lax.broadcasted_iota(jnp.int32, (n, n), 1)

    def add(k, total):
        at = pl.multiple_of(k * n, n)
        onehot = jnp.where(places == column + at, 1.0, 0.0).astype(BF)
        return total + jnp.dot(onehot, rows_ref[pl.ds(at, n), :], preferred_element_type=F32)

    total = jnp.zeros((n, rows_ref.shape[1]), F32)
    total = lax.fori_loop(0, rows_ref.shape[0] // n, add, total)
    unit = total * lax.rsqrt(jnp.sum(total * total, axis=1, keepdims=True) + EPSILON)
    out_ref[:n, :] = unit.astype(BF)
    out_ref[n:, :] = extra_ref[...]


def pick(rows, owner, extra):
    n = owner.shape[1]
    return vmem_call(
        pick_kernel,
        jax.ShapeDtypeStruct((n + extra.shape[0], rows.shape[1]), BF),
        "pick",
        in_specs=[IN_VMEM] * 3,
        out_specs=IN_VMEM,
    )(rows, owner, extra)


def exps_kernel(a_ref, *refs):
    views, (e_ref, t_ref) = refs[:NZ], refs[NZ:]
    n = t_ref.shape[1]
    a = a_ref[:n, :]
    total = jnp.zeros((8, n), F32)
    for k in range(NZ):
        dots = lax.dot_general(
            views[k][...], a, (((1,), (1,)), ((), ())), preferred_element_type=F32
        )
        e = jnp.exp2(dots * EXPONENT)
        total = total + jnp.sum(e.reshape(n // 8, 8, n), axis=0)
        e_ref[k] = e.astype(BF)
    t_ref[...] = jnp.sum(total, axis=0, keepdims=True)


def exps(anchors, views):
    n = views[0].shape[0]
    return vmem_call(
        exps_kernel,
        (jax.ShapeDtypeStruct((NZ, n, n), BF), jax.ShapeDtypeStruct((1, n), F32)),
        "exps",
        in_specs=[IN_VMEM] * (1 + NZ),
        out_specs=(IN_VMEM, IN_VMEM),
    )(anchors, *views)


def weights_of(message_ref, n):
    w = message_ref[n : n + 16, :].astype(F32)
    return jnp.concatenate([w[k : k + 1, :] for k in range(n // w.shape[1])], axis=1)


def scale_kernel(*refs):
    anchors = refs[:NX]
    totals = refs[NX : 2 * NX]
    out_ref = refs[2 * NX]
    n = out_ref.shape[0] // NX
    for b in range(NX):
        t = None
        for k in range(NX):
            at = ((b - k) % NX) * n
            piece = totals[k][:, at : at + n]
            t = piece if t is None else t + piece
        column = column_of((1.0 / TEMPER) * weights_of(anchors[b], n) / t)
        out_ref[b * n : (b + 1) * n, :] = (anchors[b][:n, :].astype(F32) * column).astype(BF)


def scale(anchors, totals, n):
    return vmem_call(
        scale_kernel,
        jax.ShapeDtypeStruct((NX * n, anchors[0].shape[1]), BF),
        "scale",
        in_specs=[IN_VMEM] * (2 * NX),
        out_specs=IN_VMEM,
    )(*anchors, *totals)


def mix_kernel(a_ref, *refs):
    parts = refs[:NX]
    out_ref, far0_ref, far1_ref, up_ref, down_ref = refs[NX:]
    half = far0_ref.shape[0]

    def one(k, carry):
        total = None
        for b, part in enumerate(parts):
            size = part.shape[2]
            term = jnp.dot(part[k], a_ref[b * size : (b + 1) * size, :], preferred_element_type=F32)
            total = term if total is None else total + term
        out_ref[k] = total
        return carry

    lax.fori_loop(0, NZ, one, 0)
    far = NZ // 2
    far0_ref[...] = out_ref[far, :half].astype(BF)
    far1_ref[...] = out_ref[far, half:].astype(BF)
    up_ref[...] = out_ref[far - 1, half:].astype(BF)
    down_ref[...] = out_ref[far + 1, :half].astype(BF)


def mix(scaled, parts):
    n, width = parts[0].shape[1], scaled.shape[1]
    half = jax.ShapeDtypeStruct((n // 2, width), BF)
    return vmem_call(
        mix_kernel,
        (jax.ShapeDtypeStruct((NZ, n, width), F32), half, half, half, half),
        "mix",
        in_specs=[IN_VMEM] * (1 + NX),
        out_specs=(IN_VMEM,) * 5,
    )(scaled, *parts)


def finish_kernel(core_ref, *refs):
    halves, own_ref = refs[:4], refs[4]
    message_ref, feats_ref, weight_ref, grad_ref, keep_ref, send_ref, part_ref = refs[5:]
    n = feats_ref.shape[0]
    feats = feats_ref[...]
    unit, inv = project(feats, weight_ref[...])
    mixed = own_ref[...] + jnp.concatenate(
        [halves[h][...].astype(F32) + halves[2 + h][...].astype(F32) for h in range(2)], axis=0
    )
    w = column_of((1.0 / TEMPER) * weights_of(message_ref, n))
    grad = mixed - w * message_ref[:n, :].astype(F32)
    along = jnp.sum(unit * grad, axis=1, keepdims=True)
    grad = ((grad - unit * along) * inv).astype(BF)
    grad_ref[...] = grad
    part_ref[...] = lax.dot_general(
        feats, grad, (((0,), (0,)), ((), ())), preferred_element_type=F32
    )
    half = keep_ref.shape[0]
    core = core_ref[0]
    keep_ref[...] = part_ref[pl.ds(pl.multiple_of(core * half, half), half), :]
    send_ref[...] = part_ref[pl.ds(pl.multiple_of((NC - 1 - core) * half, half), half), :]


def finish(core, ups, downs, own, message, features, weight):
    n, width = features.shape[0], weight.shape[1]
    half = jax.ShapeDtypeStruct((features.shape[1] // NC, width), F32)
    return vmem_call(
        finish_kernel,
        (jax.ShapeDtypeStruct((n, width), BF), half, half),
        "finish",
        in_specs=[pl.BlockSpec(memory_space=pltpu.SMEM)] + [IN_VMEM] * 8,
        out_specs=(IN_VMEM,) * 3,
        scratch_shapes=[pltpu.VMEM((features.shape[1], width), F32)],
    )(core.reshape(1), *ups, *downs, own, message, features, weight)


def sum_everywhere(keep, send, core, beside):
    rows, width = keep.shape
    v = keep + lax.ppermute(send, "core", flip(NC, 1))
    many = NY * NX
    v = lax.all_to_all(v.astype(BF), ("y", "x"), 0, 0, tiled=True).astype(F32)
    v = jnp.sum(v.reshape(many, rows // many, width), axis=0)
    got = [lax.ppermute(v, "z", flip(NZ, m)) for m in (1, 2, 3)]
    v = (v + got[0]) + (got[1] + got[2])
    v = v + lax.ppermute(v, "z", flip(NZ, 4))
    v, beside = lax.optimization_barrier((v.astype(BF), beside))
    v = lax.optimization_barrier(jnp.broadcast_to(v[None], (many,) + v.shape))
    v = lax.all_to_all(v.reshape(rows, width), ("y", "x"), 0, 0, tiled=True)
    other = lax.ppermute(v, "core", flip(NC, 1))
    low, high = jnp.where(core == 0, v, other), jnp.where(core == 0, other, v)
    return jnp.concatenate([low, high], axis=0).astype(F32), beside


def local(features, weight, support_queue, owner_shard, slot_row, loss_weight):
    n = features.shape[0]
    width = weight.shape[1]

    core = lax.axis_index("core")
    owner = owner_shard.reshape(1, n)
    view_bf, wanted = begin(features, weight, owner, slot_row.reshape(1, n))
    views = {0: view_bf}
    views[7] = lax.ppermute(view_bf, "z", shift(NZ, 1))
    views[1] = lax.ppermute(view_bf, "z", shift(NZ, -1))
    asked = lax.all_to_all(wanted, QUEUE, split_axis=0, concat_axis=0, tiled=True)
    asked, views[7], views[1] = lax.optimization_barrier((asked, views[7], views[1]))
    views[6] = lax.ppermute(views[7], "z", shift(NZ, 1))
    views[2] = lax.ppermute(views[1], "z", shift(NZ, -1))
    picked = support_queue[asked]
    picked, views[6], views[2] = lax.optimization_barrier((picked, views[6], views[2]))
    views[5] = lax.ppermute(views[6], "z", shift(NZ, 1))
    views[3] = lax.ppermute(views[2], "z", shift(NZ, -1))
    views[4] = lax.ppermute(views[5], "z", shift(NZ, 1))
    views = [views[d] for d in range(NZ)]

    answered = lax.all_to_all(picked, QUEUE, split_axis=0, concat_axis=0, tiled=True)
    extra = jnp.zeros((16, width), BF).at[: n // width].set(loss_weight.reshape(n // width, width))
    message = pick(answered.reshape(NZ * NX * CAP, width), owner, extra)

    blocks = [message] + [lax.ppermute(message, "x", shift(NX, k)) for k in (1, 2, 3)]
    parts, totals = {}, {}
    for b in (0, 1, 3, 2):
        parts[b], totals[b] = exps(blocks[b], views)
    parts = [parts[b] for b in range(NX)]
    total = jnp.concatenate([totals[b] for b in range(NX)], axis=1)
    everyone = [total] + [lax.ppermute(total, "x", shift(NX, k)) for k in (1, 2, 3)]
    scaled = scale(blocks, everyone, n)

    def hop(v, by, part):
        return (lax.ppermute(v, "z", shift(NZ, by)).astype(F32) + part).astype(BF)

    half = n // 2
    mixed, far0, far1, up1, down0 = mix(scaled, parts)
    own = mixed[0]
    piece = {(d, h): mixed[d, h * half : (h + 1) * half] for d in (1, 2, 6, 7) for h in range(2)}
    piece[3, 0], piece[5, 1] = mixed[3, :half], mixed[5, half:]
    own, piece = lax.optimization_barrier((own, piece))
    ups, downs = [hop(far0, 1, piece[3, 0]), up1], [down0, hop(far1, -1, piece[5, 1])]
    for d in (2, 1):
        ups = [hop(v, 1, piece[d, h]) for h, v in enumerate(ups)]
        downs = [hop(v, -1, piece[NZ - d, h]) for h, v in enumerate(downs)]
    ups = [lax.ppermute(v, "z", shift(NZ, 1)) for v in ups]
    downs = [lax.ppermute(v, "z", shift(NZ, -1)) for v in downs]

    grad_proj, keep, send = finish(core, ups, downs, own, message, features, weight)
    grad_feats = jnp.dot(grad_proj, weight.T, preferred_element_type=F32).astype(BF)
    grad_weight, grad_feats = sum_everywhere(keep, send, core, grad_feats)
    return (grad_feats, grad_weight)


def solution(mesh):
    mesh = Mesh(mesh.devices.reshape(NY, NC, NZ, NX), ("y", "core", "z", "x"))
    views = ("y", "core", "z", "x")
    in_specs = (
        P(views, None),
        P(),
        P(QUEUE, None),
        P(views, None),
        P(views),
        P(views),
    )
    out_specs = (P(views, None), P())
    return jax.shard_map(local, mesh=mesh, in_specs=in_specs, out_specs=out_specs, check_vma=False)
```

```python
import functools
import math

import jax
import jax.numpy as jnp
from jax import lax
from jax.experimental import pallas as pl
from jax.experimental.pallas import tpu as pltpu
from jax.sharding import Mesh
from jax.sharding import PartitionSpec as P

TEMPER = 0.1
EPSILON = 1e-06
NZ, NX, NY, NC = 8, 4, 4, 2
CAP = 64
BF = jnp.bfloat16
F32 = jnp.float32
VMEM_LIMIT = 16 * 1024 * 1024
ALL_VMEM = 62 * 1024 * 1024
IN_VMEM = pl.BlockSpec(memory_space=pltpu.VMEM)
EXPONENT = math.log2(math.e) / TEMPER
QUEUE = ("z", "x")


def shift(size, by):
    return [(i, (i + by) % size) for i in range(size)]


def flip(size, mask):
    return [(i, i ^ mask) for i in range(size)]


def vmem_call(kernel, out_shape, name, limit=VMEM_LIMIT, **kw):
    return pl.pallas_call(
        kernel,
        out_shape=out_shape,
        compiler_params=pltpu.CompilerParams(vmem_limit_bytes=limit),
        name=name,
        **kw,
    )


def ranks(owner, shards):
    n = owner.shape[1]
    onehot = jnp.where(owner == lax.broadcasted_iota(jnp.int32, (shards, n), 0), 1.0, 0.0)
    above = lax.broadcasted_iota(jnp.int32, (n, n), 0) < lax.broadcasted_iota(jnp.int32, (n, n), 1)
    above = jnp.where(above, 1.0, 0.0).astype(BF)
    before = jnp.dot(onehot.astype(BF), above, preferred_element_type=F32)
    return onehot, jnp.sum(before * onehot, axis=0, keepdims=True).astype(jnp.int32)


def project(features, weight):
    projected = jnp.dot(features, weight, preferred_element_type=F32)
    inv = lax.rsqrt(jnp.sum(projected * projected, axis=1, keepdims=True) + EPSILON)
    return projected * inv, inv


def begin_kernel(
    feats_hbm,
    weight_hbm,
    owner_hbm,
    slot_hbm,
    view_ref,
    wanted_ref,
    feats_ref,
    weight_ref,
    owner_ref,
    slot_ref,
    sems,
):
    copies = [
        pltpu.make_async_copy(owner_hbm, owner_ref, sems.at[0]),
        pltpu.make_async_copy(slot_hbm, slot_ref, sems.at[1]),
        pltpu.make_async_copy(weight_hbm, weight_ref, sems.at[2]),
        pltpu.make_async_copy(feats_hbm, feats_ref, sems.at[3]),
    ]
    for copy in copies:
        copy.start()
    copies[0].wait()
    copies[1].wait()
    n = owner_ref.shape[1]
    slot = slot_ref[...]
    onehot, rank = ranks(owner_ref[...], wanted_ref.shape[0])
    chosen = jnp.where(rank == lax.broadcasted_iota(jnp.int32, (128, n), 0), 1.0, 0.0).astype(BF)
    both = (((1,), (1,)), ((), ()))
    high = (onehot * (slot >> 7).astype(F32)).astype(BF)
    low = (onehot * (slot & 127).astype(F32)).astype(BF)
    upper = lax.dot_general(high, chosen, both, preferred_element_type=F32)
    lower = lax.dot_general(low, chosen, both, preferred_element_type=F32)
    full = upper.astype(jnp.int32) * 128 + lower.astype(jnp.int32)
    wanted_ref[...] = full[:, :CAP]
    copies[2].wait()
    copies[3].wait()
    view_ref[...] = project(feats_ref[...], weight_ref[...])[0].astype(BF)


def begin(features, weight, owner, slot):
    n, width = features.shape[0], weight.shape[1]
    in_hbm = pl.BlockSpec(memory_space=pltpu.HBM)
    return vmem_call(
        begin_kernel,
        (
            jax.ShapeDtypeStruct((n, width), BF),
            jax.ShapeDtypeStruct((NZ * NX, CAP), jnp.int32),
        ),
        "begin",
        ALL_VMEM,
        in_specs=[in_hbm] * 4,
        out_specs=(IN_VMEM, IN_VMEM),
        scratch_shapes=[
            pltpu.VMEM(features.shape, BF),
            pltpu.VMEM(weight.shape, BF),
            pltpu.VMEM(owner.shape, jnp.int32),
            pltpu.VMEM(slot.shape, jnp.int32),
            pltpu.SemaphoreType.DMA((4,)),
        ],
    )(features, weight, owner, slot)


def column_of(row):
    return jnp.broadcast_to(row, (8, row.shape[1])).T[:, :1]


def pick_kernel(rows_ref, owner_ref, extra_ref, out_ref):
    n = owner_ref.shape[1]
    owner = owner_ref[...]
    places = column_of(owner * CAP + ranks(owner, rows_ref.shape[0] // CAP)[1])
    column = lax.broadcasted_iota(jnp.int32, (n, n), 1)
    total = None
    for at in range(0, rows_ref.shape[0], n):
        onehot = jnp.where(places == column + at, 1.0, 0.0).astype(BF)
        term = jnp.dot(onehot, rows_ref[at : at + n, :], preferred_element_type=F32)
        total = term if total is None else total + term
    unit = total * lax.rsqrt(jnp.sum(total * total, axis=1, keepdims=True) + EPSILON)
    out_ref[:n, :] = unit.astype(BF)
    out_ref[n:, :] = extra_ref[...]


def pick(rows, owner, extra):
    n = owner.shape[1]
    return vmem_call(
        pick_kernel,
        jax.ShapeDtypeStruct((n + extra.shape[0], rows.shape[1]), BF),
        "pick",
        in_specs=[IN_VMEM] * 3,
        out_specs=IN_VMEM,
    )(rows, owner, extra)


def exps_kernel(a_ref, *refs):
    views, (e_ref, t_ref) = refs[:NZ], refs[NZ:]
    n = t_ref.shape[1]
    a = a_ref[:n, :]
    half = n // 2

    def part(h, total):
        rows = pl.ds(pl.multiple_of(h * half, half), half)
        for k in range(NZ):
            dots = lax.dot_general(
                views[k][rows, :], a, (((1,), (1,)), ((), ())), preferred_element_type=F32
            )
            e = jnp.exp2(dots * EXPONENT)
            total = total + jnp.sum(e.reshape(half // 8, 8, n), axis=0)
            e_ref[k, rows, :] = e.astype(BF)
        return total

    total = lax.fori_loop(0, 2, part, jnp.zeros((8, n), F32))
    t_ref[...] = jnp.sum(total, axis=0, keepdims=True)


def exps(anchors, views):
    n = views[0].shape[0]
    return vmem_call(
        exps_kernel,
        (jax.ShapeDtypeStruct((NZ, n, n), BF), jax.ShapeDtypeStruct((1, n), F32)),
        "exps",
        in_specs=[IN_VMEM] * (1 + NZ),
        out_specs=(IN_VMEM, IN_VMEM),
    )(anchors, *views)


def weights_of(message_ref, n):
    w = message_ref[n : n + 16, :].astype(F32)
    return jnp.concatenate([w[k : k + 1, :] for k in range(n // w.shape[1])], axis=1)


def scale_kernel(*refs):
    anchors = refs[:NX]
    totals = refs[NX : 2 * NX]
    out_ref = refs[2 * NX]
    n = out_ref.shape[0] // NX
    for b in range(NX):
        t = None
        for k in range(NX):
            at = ((b - k) % NX) * n
            piece = totals[k][:, at : at + n]
            t = piece if t is None else t + piece
        column = column_of((1.0 / TEMPER) * weights_of(anchors[b], n) / t)
        out_ref[b * n : (b + 1) * n, :] = (anchors[b][:n, :].astype(F32) * column).astype(BF)


def scale(anchors, totals, n):
    return vmem_call(
        scale_kernel,
        jax.ShapeDtypeStruct((NX * n, anchors[0].shape[1]), BF),
        "scale",
        in_specs=[IN_VMEM] * (2 * NX),
        out_specs=IN_VMEM,
    )(*anchors, *totals)


def product(k, a_ref, parts):
    total = None
    for b, part in enumerate(parts):
        size = part.shape[2]
        term = jnp.dot(part[k], a_ref[b * size : (b + 1) * size, :], preferred_element_type=F32)
        total = term if total is None else total + term
    return total


def mix_kernel(which, a_ref, *refs):
    outs = iter(refs[NX:])
    for k in which:
        total = product(k, a_ref, refs[:NX])
        half = total.shape[0] // 2
        for h in range(2):
            out = next(outs)
            out[...] = total[h * half : (h + 1) * half].astype(out.dtype)


def mix(which, scaled, parts, dtype):
    shape = jax.ShapeDtypeStruct((parts[0].shape[1] // 2, scaled.shape[1]), dtype)
    return vmem_call(
        functools.partial(mix_kernel, which),
        (shape,) * (2 * len(which)),
        "mix",
        in_specs=[IN_VMEM] * (1 + NX),
        out_specs=(IN_VMEM,) * (2 * len(which)),
    )(scaled, *parts)


def finish_kernel(core_ref, *refs):
    halves, (*others, part_ref) = refs[:6], refs[6:]
    message_ref, feats_ref, weight_ref, grad_ref, keep_ref, send_ref = others
    n = feats_ref.shape[0]
    feats = feats_ref[...]
    unit, inv = project(feats, weight_ref[...])
    mixed = jnp.concatenate(
        [sum(halves[2 * k + h][...].astype(F32) for k in range(3)) for h in range(2)], axis=0
    )
    w = column_of((1.0 / TEMPER) * weights_of(message_ref, n))
    grad = mixed - w * message_ref[:n, :].astype(F32)
    along = jnp.sum(unit * grad, axis=1, keepdims=True)
    grad = ((grad - unit * along) * inv).astype(BF)
    grad_ref[...] = grad
    part_ref[...] = lax.dot_general(
        feats, grad, (((0,), (0,)), ((), ())), preferred_element_type=F32
    )
    half = keep_ref.shape[0]
    core = core_ref[0]
    keep_ref[...] = part_ref[pl.ds(pl.multiple_of(core * half, half), half), :]
    send_ref[...] = part_ref[pl.ds(pl.multiple_of((NC - 1 - core) * half, half), half), :]


def finish(core, ups, downs, own, message, features, weight):
    n, width = features.shape[0], weight.shape[1]
    half = jax.ShapeDtypeStruct((features.shape[1] // NC, width), F32)
    return vmem_call(
        finish_kernel,
        (jax.ShapeDtypeStruct((n, width), BF), half, half),
        "finish",
        in_specs=[pl.BlockSpec(memory_space=pltpu.SMEM)] + [IN_VMEM] * 9,
        out_specs=(IN_VMEM,) * 3,
        scratch_shapes=[pltpu.VMEM((features.shape[1], width), F32)],
    )(core.reshape(1), *own, *ups, *downs, message, features, weight)


def sum_everywhere(keep, send, core, beside):
    rows, width = keep.shape
    v = keep + lax.ppermute(send, "core", flip(NC, 1))
    many = NY * NX
    v = lax.all_to_all(v.astype(BF), ("y", "x"), 0, 0, tiled=True).astype(F32)
    v = jnp.sum(v.reshape(many, rows // many, width), axis=0)
    got = [lax.ppermute(v, "z", flip(NZ, m)) for m in (1, 2, 3)]
    v = (v + got[0]) + (got[1] + got[2])
    v = v + lax.ppermute(v, "z", flip(NZ, 4))
    v, beside = lax.optimization_barrier((v.astype(BF), beside))
    v = lax.optimization_barrier(jnp.broadcast_to(v[None], (many,) + v.shape))
    v = lax.all_to_all(v.reshape(rows, width), ("y", "x"), 0, 0, tiled=True)
    other = lax.ppermute(v, "core", flip(NC, 1))
    low, high = jnp.where(core == 0, v, other), jnp.where(core == 0, other, v)
    return jnp.concatenate([low, high], axis=0).astype(F32), beside


def local(features, weight, support_queue, owner_shard, slot_row, loss_weight):
    n = features.shape[0]
    width = weight.shape[1]

    core = lax.axis_index("core")
    owner = owner_shard.reshape(1, n)
    view_bf, wanted = begin(features, weight, owner, slot_row.reshape(1, n))
    views = {0: view_bf}
    views[7] = lax.ppermute(view_bf, "z", shift(NZ, 1))
    views[1] = lax.ppermute(view_bf, "z", shift(NZ, -1))
    asked = lax.all_to_all(wanted, QUEUE, split_axis=0, concat_axis=0, tiled=True)
    asked, views[7], views[1] = lax.optimization_barrier((asked, views[7], views[1]))
    views[6] = lax.ppermute(views[7], "z", shift(NZ, 1))
    views[2] = lax.ppermute(views[1], "z", shift(NZ, -1))
    picked = support_queue[asked]
    picked, views[6], views[2] = lax.optimization_barrier((picked, views[6], views[2]))
    views[5] = lax.ppermute(views[6], "z", shift(NZ, 1))
    views[3] = lax.ppermute(views[2], "z", shift(NZ, -1))
    views[4] = lax.ppermute(views[5], "z", shift(NZ, 1))
    views = [views[d] for d in range(NZ)]

    answered = lax.all_to_all(picked, QUEUE, split_axis=0, concat_axis=0, tiled=True)
    extra = jnp.zeros((16, width), BF).at[: n // width].set(loss_weight.reshape(n // width, width))
    message = pick(answered.reshape(NZ * NX * CAP, width), owner, extra)

    blocks = [message] + [lax.ppermute(message, "x", shift(NX, k)) for k in (1, 2, 3)]
    parts, totals = {}, {}
    for b in (0, 1, 3, 2):
        parts[b], totals[b] = exps(blocks[b], views)
    parts = [parts[b] for b in range(NX)]
    total = jnp.concatenate([totals[b] for b in range(NX)], axis=1)
    everyone = [total] + [lax.ppermute(total, "x", shift(NX, k)) for k in (1, 2, 3)]
    scaled = scale(blocks, everyone, n)

    def hop(v, by, part):
        return (lax.ppermute(v, "z", shift(NZ, by)).astype(F32) + part).astype(BF)

    far = mix((NZ // 2,), scaled, parts, BF)
    up0, up1, down0, down1 = mix((3, NZ - 3), scaled, parts, F32)
    ups, downs = [hop(far[0], 1, up0), up1.astype(BF)], [down0.astype(BF), hop(far[1], -1, down1)]
    for d in (2, 1):
        which = (d, NZ - d) if d > 1 else (d, NZ - d, 0)
        up0, up1, down0, down1, *own = mix(which, scaled, parts, F32)
        ups = [hop(ups[0], 1, up0), hop(ups[1], 1, up1)]
        downs = [hop(downs[0], -1, down0), hop(downs[1], -1, down1)]
    ups = [lax.ppermute(v, "z", shift(NZ, 1)) for v in ups]
    downs = [lax.ppermute(v, "z", shift(NZ, -1)) for v in downs]

    grad_proj, keep, send = finish(core, ups, downs, own, message, features, weight)
    grad_feats = jnp.dot(grad_proj, weight.T, preferred_element_type=F32).astype(BF)
    grad_weight, grad_feats = sum_everywhere(keep, send, core, grad_feats)
    return (grad_feats, grad_weight)


def solution(mesh):
    mesh = Mesh(mesh.devices.reshape(NY, NC, NZ, NX), ("y", "core", "z", "x"))
    views = ("y", "core", "z", "x")
    in_specs = (
        P(views, None),
        P(),
        P(QUEUE, None),
        P(views, None),
        P(views),
        P(views),
    )
    out_specs = (P(views, None), P())
    return jax.shard_map(local, mesh=mesh, in_specs=in_specs, out_specs=out_specs, check_vma=False)
```

```python
import functools
import math

import jax
import jax.numpy as jnp
from jax import lax
from jax.experimental import pallas as pl
from jax.experimental.pallas import tpu as pltpu
from jax.sharding import Mesh
from jax.sharding import PartitionSpec as P

TEMPER = 0.1
EPSILON = 1e-06
NZ, NX, NY, NC = 8, 4, 4, 2
CAP = 64
BF = jnp.bfloat16
F32 = jnp.float32
VMEM_LIMIT = 16 * 1024 * 1024
ALL_VMEM = 62 * 1024 * 1024
IN_VMEM = pl.BlockSpec(memory_space=pltpu.VMEM)
EXPONENT = math.log2(math.e) / TEMPER
QUEUE = ("z", "x")


def shift(size, by):
    return [(i, (i + by) % size) for i in range(size)]


def flip(size, mask):
    return [(i, i ^ mask) for i in range(size)]


def vmem_call(kernel, out_shape, name, limit=VMEM_LIMIT, **kw):
    return pl.pallas_call(
        kernel,
        out_shape=out_shape,
        compiler_params=pltpu.CompilerParams(vmem_limit_bytes=limit),
        name=name,
        **kw,
    )


def ranks(owner, shards):
    n = owner.shape[1]
    onehot = jnp.where(owner == lax.broadcasted_iota(jnp.int32, (shards, n), 0), 1.0, 0.0)
    above = lax.broadcasted_iota(jnp.int32, (n, n), 0) < lax.broadcasted_iota(jnp.int32, (n, n), 1)
    above = jnp.where(above, 1.0, 0.0).astype(BF)
    before = jnp.dot(onehot.astype(BF), above, preferred_element_type=F32)
    return onehot, jnp.sum(before * onehot, axis=0, keepdims=True).astype(jnp.int32)


def project(features, weight):
    projected = jnp.dot(features, weight, preferred_element_type=F32)
    inv = lax.rsqrt(jnp.sum(projected * projected, axis=1, keepdims=True) + EPSILON)
    return projected * inv, inv


def begin_kernel(
    feats_hbm,
    weight_hbm,
    owner_hbm,
    slot_hbm,
    view_ref,
    wanted_ref,
    feats_ref,
    weight_ref,
    owner_ref,
    slot_ref,
    sems,
):
    copies = [
        pltpu.make_async_copy(owner_hbm, owner_ref, sems.at[0]),
        pltpu.make_async_copy(slot_hbm, slot_ref, sems.at[1]),
        pltpu.make_async_copy(weight_hbm, weight_ref, sems.at[2]),
        pltpu.make_async_copy(feats_hbm, feats_ref, sems.at[3]),
    ]
    for copy in copies:
        copy.start()
    copies[0].wait()
    copies[1].wait()
    n = owner_ref.shape[1]
    slot = slot_ref[...]
    onehot, rank = ranks(owner_ref[...], wanted_ref.shape[0])
    chosen = jnp.where(rank == lax.broadcasted_iota(jnp.int32, (128, n), 0), 1.0, 0.0).astype(BF)
    both = (((1,), (1,)), ((), ()))
    high = (onehot * (slot >> 7).astype(F32)).astype(BF)
    low = (onehot * (slot & 127).astype(F32)).astype(BF)
    upper = lax.dot_general(high, chosen, both, preferred_element_type=F32)
    lower = lax.dot_general(low, chosen, both, preferred_element_type=F32)
    full = upper.astype(jnp.int32) * 128 + lower.astype(jnp.int32)
    wanted_ref[...] = full[:, :CAP]
    copies[2].wait()
    copies[3].wait()
    view_ref[...] = project(feats_ref[...], weight_ref[...])[0].astype(BF)


def begin(features, weight, owner, slot):
    n, width = features.shape[0], weight.shape[1]
    in_hbm = pl.BlockSpec(memory_space=pltpu.HBM)
    return vmem_call(
        begin_kernel,
        (
            jax.ShapeDtypeStruct((n, width), BF),
            jax.ShapeDtypeStruct((NZ * NX, CAP), jnp.int32),
        ),
        "begin",
        ALL_VMEM,
        in_specs=[in_hbm] * 4,
        out_specs=(IN_VMEM, IN_VMEM),
        scratch_shapes=[
            pltpu.VMEM(features.shape, BF),
            pltpu.VMEM(weight.shape, BF),
            pltpu.VMEM(owner.shape, jnp.int32),
            pltpu.VMEM(slot.shape, jnp.int32),
            pltpu.SemaphoreType.DMA((4,)),
        ],
    )(features, weight, owner, slot)


def column_of(row):
    return jnp.broadcast_to(row, (8, row.shape[1])).T[:, :1]


def pick_kernel(rows_ref, owner_ref, extra_ref, out_ref):
    n = owner_ref.shape[1]
    owner = owner_ref[...]
    places = column_of(owner * CAP + ranks(owner, rows_ref.shape[0] // CAP)[1])
    column = lax.broadcasted_iota(jnp.int32, (n, n), 1)
    total = None
    for at in range(0, rows_ref.shape[0], n):
        onehot = jnp.where(places == column + at, 1.0, 0.0).astype(BF)
        term = jnp.dot(onehot, rows_ref[at : at + n, :], preferred_element_type=F32)
        total = term if total is None else total + term
    unit = total * lax.rsqrt(jnp.sum(total * total, axis=1, keepdims=True) + EPSILON)
    out_ref[:n, :] = unit.astype(BF)
    out_ref[n:, :] = extra_ref[...]


def pick(rows, owner, extra):
    n = owner.shape[1]
    return vmem_call(
        pick_kernel,
        jax.ShapeDtypeStruct((n + extra.shape[0], rows.shape[1]), BF),
        "pick",
        in_specs=[IN_VMEM] * 3,
        out_specs=IN_VMEM,
    )(rows, owner, extra)


def exps_kernel(a_ref, *refs):
    views, (e_ref, t_ref) = refs[:NZ], refs[NZ:]
    n = t_ref.shape[1]
    a = a_ref[:n, :]
    half = n // 2

    def part(h, total):
        rows = pl.ds(pl.multiple_of(h * half, half), half)
        for k in range(NZ):
            dots = lax.dot_general(
                views[k][rows, :], a, (((1,), (1,)), ((), ())), preferred_element_type=F32
            )
            e = jnp.exp2(dots * EXPONENT)
            total = total + jnp.sum(e.reshape(half // 8, 8, n), axis=0)
            e_ref[k, rows, :] = e.astype(BF)
        return total

    total = lax.fori_loop(0, 2, part, jnp.zeros((8, n), F32))
    t_ref[...] = jnp.sum(total, axis=0, keepdims=True)


def exps(anchors, views):
    n = views[0].shape[0]
    return vmem_call(
        exps_kernel,
        (jax.ShapeDtypeStruct((NZ, n, n), BF), jax.ShapeDtypeStruct((1, n), F32)),
        "exps",
        in_specs=[IN_VMEM] * (1 + NZ),
        out_specs=(IN_VMEM, IN_VMEM),
    )(anchors, *views)


def weights_of(message_ref, n):
    w = message_ref[n : n + 16, :].astype(F32)
    return jnp.concatenate([w[k : k + 1, :] for k in range(n // w.shape[1])], axis=1)


def scale_kernel(*refs):
    anchors = refs[:NX]
    totals = refs[NX : 2 * NX]
    out_ref = refs[2 * NX]
    n = out_ref.shape[0] // NX
    for b in range(NX):
        t = None
        for k in range(NX):
            at = ((b - k) % NX) * n
            piece = totals[k][:, at : at + n]
            t = piece if t is None else t + piece
        column = column_of((1.0 / TEMPER) * weights_of(anchors[b], n) / t)
        out_ref[b * n : (b + 1) * n, :] = (anchors[b][:n, :].astype(F32) * column).astype(BF)


def scale(anchors, totals, n):
    return vmem_call(
        scale_kernel,
        jax.ShapeDtypeStruct((NX * n, anchors[0].shape[1]), BF),
        "scale",
        in_specs=[IN_VMEM] * (2 * NX),
        out_specs=IN_VMEM,
    )(*anchors, *totals)


def product(k, a_ref, parts):
    total = None
    for b, part in enumerate(parts):
        size = part.shape[2]
        term = jnp.dot(part[k], a_ref[b * size : (b + 1) * size, :], preferred_element_type=F32)
        total = term if total is None else total + term
    return total


def mix_kernel(which, a_ref, *refs):
    outs = iter(refs[NX:])
    for k in which:
        total = product(k, a_ref, refs[:NX])
        half = total.shape[0] // 2
        for h in range(2):
            out = next(outs)
            out[...] = total[h * half : (h + 1) * half].astype(out.dtype)


def mix(which, scaled, parts, dtype):
    shape = jax.ShapeDtypeStruct((parts[0].shape[1] // 2, scaled.shape[1]), dtype)
    return vmem_call(
        functools.partial(mix_kernel, which),
        (shape,) * (2 * len(which)),
        "mix",
        in_specs=[IN_VMEM] * (1 + NX),
        out_specs=(IN_VMEM,) * (2 * len(which)),
    )(scaled, *parts)


def finish_kernel(core_ref, *refs):
    halves, (*others, part_ref) = refs[:6], refs[6:]
    message_ref, feats_ref, weight_ref, grad_ref, keep_ref, send_ref = others
    n = feats_ref.shape[0]
    feats = feats_ref[...]
    unit, inv = project(feats, weight_ref[...])
    mixed = jnp.concatenate(
        [sum(halves[2 * k + h][...].astype(F32) for k in range(3)) for h in range(2)], axis=0
    )
    w = column_of((1.0 / TEMPER) * weights_of(message_ref, n))
    grad = mixed - w * message_ref[:n, :].astype(F32)
    along = jnp.sum(unit * grad, axis=1, keepdims=True)
    grad = ((grad - unit * along) * inv).astype(BF)
    grad_ref[...] = grad
    part_ref[...] = lax.dot_general(
        feats, grad, (((0,), (0,)), ((), ())), preferred_element_type=F32
    )
    half = keep_ref.shape[0]
    core = core_ref[0]
    keep_ref[...] = part_ref[pl.ds(pl.multiple_of(core * half, half), half), :]
    send_ref[...] = part_ref[pl.ds(pl.multiple_of((NC - 1 - core) * half, half), half), :]


def finish(core, ups, downs, own, message, features, weight):
    n, width = features.shape[0], weight.shape[1]
    half = jax.ShapeDtypeStruct((features.shape[1] // NC, width), F32)
    return vmem_call(
        finish_kernel,
        (jax.ShapeDtypeStruct((n, width), BF), half, half),
        "finish",
        in_specs=[pl.BlockSpec(memory_space=pltpu.SMEM)] + [IN_VMEM] * 9,
        out_specs=(IN_VMEM,) * 3,
        scratch_shapes=[pltpu.VMEM((features.shape[1], width), F32)],
    )(core.reshape(1), *own, *ups, *downs, message, features, weight)


def sum_everywhere(keep, send, core, beside):
    rows, width = keep.shape
    v = keep + lax.ppermute(send, "core", flip(NC, 1))
    many = NY * NX
    v = lax.all_to_all(v.astype(BF), ("y", "x"), 0, 0, tiled=True).astype(F32)
    v = jnp.sum(v.reshape(many, rows // many, width), axis=0)
    v = lax.optimization_barrier(jnp.broadcast_to(v[None], (NZ,) + v.shape))
    v = lax.all_to_all(v.reshape(NZ * rows // many, width), "z", 0, 0, tiled=True)
    v = jnp.sum(v.reshape(NZ, rows // many, width), axis=0)
    v, beside = lax.optimization_barrier((v.astype(BF), beside))
    v = lax.optimization_barrier(jnp.broadcast_to(v[None], (many,) + v.shape))
    v = lax.all_to_all(v.reshape(rows, width), ("y", "x"), 0, 0, tiled=True)
    other = lax.ppermute(v, "core", flip(NC, 1))
    low, high = jnp.where(core == 0, v, other), jnp.where(core == 0, other, v)
    return jnp.concatenate([low, high], axis=0).astype(F32), beside


def local(features, weight, support_queue, owner_shard, slot_row, loss_weight):
    n = features.shape[0]
    width = weight.shape[1]

    core = lax.axis_index("core")
    owner = owner_shard.reshape(1, n)
    view_bf, wanted = begin(features, weight, owner, slot_row.reshape(1, n))
    views = {0: view_bf}
    views[7] = lax.ppermute(view_bf, "z", shift(NZ, 1))
    views[1] = lax.ppermute(view_bf, "z", shift(NZ, -1))
    asked = lax.all_to_all(wanted, QUEUE, split_axis=0, concat_axis=0, tiled=True)
    asked, views[7], views[1] = lax.optimization_barrier((asked, views[7], views[1]))
    views[6] = lax.ppermute(views[7], "z", shift(NZ, 1))
    views[2] = lax.ppermute(views[1], "z", shift(NZ, -1))
    picked = support_queue[asked]
    picked, views[6], views[2] = lax.optimization_barrier((picked, views[6], views[2]))
    views[5] = lax.ppermute(views[6], "z", shift(NZ, 1))
    views[3] = lax.ppermute(views[2], "z", shift(NZ, -1))
    views[4] = lax.ppermute(views[5], "z", shift(NZ, 1))
    views = [views[d] for d in range(NZ)]

    answered = lax.all_to_all(picked, QUEUE, split_axis=0, concat_axis=0, tiled=True)
    extra = jnp.zeros((16, width), BF).at[: n // width].set(loss_weight.reshape(n // width, width))
    message = pick(answered.reshape(NZ * NX * CAP, width), owner, extra)

    blocks = [message] + [lax.ppermute(message, "x", shift(NX, k)) for k in (1, 2, 3)]
    parts, totals = {}, {}
    for b in (0, 1, 3, 2):
        parts[b], totals[b] = exps(blocks[b], views)
    parts = [parts[b] for b in range(NX)]
    total = jnp.concatenate([totals[b] for b in range(NX)], axis=1)
    everyone = [total] + [lax.ppermute(total, "x", shift(NX, k)) for k in (1, 2, 3)]
    scaled = scale(blocks, everyone, n)

    def hop(v, by, part):
        return (lax.ppermute(v, "z", shift(NZ, by)).astype(F32) + part).astype(BF)

    far = mix((NZ // 2,), scaled, parts, BF)
    up0, up1, down0, down1 = mix((3, NZ - 3), scaled, parts, F32)
    ups, downs = [hop(far[0], 1, up0), up1.astype(BF)], [down0.astype(BF), hop(far[1], -1, down1)]
    for d in (2, 1):
        which = (d, NZ - d) if d > 1 else (d, NZ - d, 0)
        up0, up1, down0, down1, *own = mix(which, scaled, parts, F32)
        ups = [hop(ups[0], 1, up0), hop(ups[1], 1, up1)]
        downs = [hop(downs[0], -1, down0), hop(downs[1], -1, down1)]
    ups = [lax.ppermute(v, "z", shift(NZ, 1)) for v in ups]
    downs = [lax.ppermute(v, "z", shift(NZ, -1)) for v in downs]

    grad_proj, keep, send = finish(core, ups, downs, own, message, features, weight)
    grad_feats = jnp.dot(grad_proj, weight.T, preferred_element_type=F32).astype(BF)
    grad_weight, grad_feats = sum_everywhere(keep, send, core, grad_feats)
    return (grad_feats, grad_weight)


def solution(mesh):
    mesh = Mesh(mesh.devices.reshape(NY, NC, NZ, NX), ("y", "core", "z", "x"))
    views = ("y", "core", "z", "x")
    in_specs = (
        P(views, None),
        P(),
        P(QUEUE, None),
        P(views, None),
        P(views),
        P(views),
    )
    out_specs = (P(views, None), P())
    return jax.shard_map(local, mesh=mesh, in_specs=in_specs, out_specs=out_specs, check_vma=False)
```
